32 devices in a mesh: gx: 16 (over z, x, core), gy: 2 (over y).
Axes of the slice: x: 2, y: 2, z: 4, core: 2. Of those that a mesh axis runs over, the one named last changes fastest.
Arguments:
- velocity: float32 [3, 32, 1024, 128], P(None, 'gx', 'gy'), may hold values from -4 to 4.5, as said below
- previous: float32 [3, 32, 1024, 128], P(None, 'gx', 'gy'), may hold values from -1800 to 1800
Outputs:
- advanced: float32 [3, 32, 1024, 128], P(None, 'gx', 'gy')
The draws below stay inside these ranges and needn't reach their ends.
Inputs may be any that keep to these rules, and one draw needn't show every extreme that they name: `velocity`: each component is zero on the two walls, the first and the last wall-normal point.
All inputs are finite; a program needn't handle non-finite values.
Results may differ from the reference program's by a relative error of at most 0.0003.
Values sent between devices are 32-bit elements; how exact they have to be, the bound alone decides.
No kernel may reach another device: no remote copies, remote signals or barrier semaphores. Data moves between devices by JAX's collectives and lax.ppermute only.
A program may use at most 64 MiB of HBM per device.

```python
import jax
import jax.numpy as jnp
from jax import lax

NY = 1024
NZ = 128
NX = 32


def draw_velocity(key, part):
    angle = jnp.pi * jnp.arange(NY, dtype=jnp.float32) / (NY - 1)
    envelope = jnp.sin(angle) ** 2
    noise = jnp.clip(jax.random.normal(key, (3, NX, NY, NZ), jnp.float32), -4.0, 4.0)
    return noise * envelope[None, None, :, None]


def block_levels(rng, dims, pieces, least, high):
    factor_of = 1.0
    for dim, parts in pieces:
        draws = jax.random.uniform(jax.random.fold_in(jax.random.fold_in(rng, 6), dim), (parts,), jnp.float32, least / len(pieces), high / len(pieces))
        factor_of = factor_of * jnp.repeat(jnp.exp(draws), dims[dim] // parts).reshape((-1,) + (1,) * (len(dims) - 1 - dim))
    return factor_of


def bell_draw(key, extent, deviation, limit, shards=(), held_as=jnp.bfloat16):
    values = deviation * jax.random.normal(key, extent, jnp.float32)
    if shards:
        values = values * block_levels(key, extent, shards, -0.22, 0.18)
    return jnp.clip(values, -limit, limit).astype(held_as)


def setup_inputs(seed: int = 0) -> dict:
    keys = jax.random.split(jax.random.key(seed), 3)
    velocity = draw_velocity(jax.random.fold_in(keys[2], 71), 0)
    previous = bell_draw(keys[1], (3, NX, NY, NZ), 300.0, 1800.0, ((1, 16), (2, 2)), jnp.float32)
    return {"velocity": velocity, "previous": previous}


LENGTH_SPACING = 8.0 * 3.141592653589793 / 4096.0
SPAN_SPACING = 3.0 * 3.141592653589793 / 3072.0
VISCOSITY = 1.0 / 2000.0
TIME_STEP = 0.003
GAMMA_NOW = 5.0 / 12.0
ZETA_PAST = -17.0 / 60.0


def chebyshev_rows(total, offset, count):
    row_ids = offset + jnp.arange(count, dtype=jnp.int32)
    col_ids = jnp.arange(total, dtype=jnp.int32)
    row_angle = jnp.pi * row_ids.astype(jnp.float32) / (total - 1)
    col_angle = jnp.pi * col_ids.astype(jnp.float32) / (total - 1)
    on_diagonal = row_ids[:, None] == col_ids[None, :]
    parity = (row_ids[:, None] + col_ids[None, :]) % 2
    signs = 1.0 - 2.0 * parity.astype(jnp.float32)
    row_half = jnp.where((row_ids == 0) | (row_ids == total - 1), 0.5, 1.0).astype(jnp.float32)
    col_half = jnp.where((col_ids == 0) | (col_ids == total - 1), 0.5, 1.0).astype(jnp.float32)
    weight_ratio = signs * col_half[None, :] / row_half[:, None]
    spacing = -2.0 * jnp.sin(0.5 * (row_angle[:, None] + col_angle[None, :])) * jnp.sin(0.5 * (row_angle[:, None] - col_angle[None, :]))
    spacing_safe = jnp.where(on_diagonal, 1.0, spacing)
    first_off = jnp.where(on_diagonal, 0.0, weight_ratio / spacing_safe)
    first_diag = -jnp.sum(first_off, axis=1)
    first = first_off + jnp.where(on_diagonal, first_diag[:, None], 0.0)
    second_off = jnp.where(on_diagonal, 0.0, 2.0 * first_off * (first_diag[:, None] - 1.0 / spacing_safe))
    second = second_off + jnp.where(on_diagonal, -jnp.sum(second_off, axis=1)[:, None], 0.0)
    return first, second


def central(center, plus_one, minus_one, plus_two, minus_two, spacing):
    first = (8.0 * (plus_one - minus_one) - (plus_two - minus_two)) / (12.0 * spacing)
    second = (16.0 * (plus_one + minus_one) - (plus_two + minus_two) - 30.0 * center) / (12.0 * spacing * spacing)
    return first, second


def periodic(field, axis, spacing):
    return central(field, jnp.roll(field, -1, axis), jnp.roll(field, 1, axis),
                   jnp.roll(field, -2, axis), jnp.roll(field, 2, axis), spacing)


def reference(velocity, previous):
    first_matrix, second_matrix = chebyshev_rows(NY, 0, NY)
    operators = jnp.concatenate([first_matrix, second_matrix], axis=0)
    results = []
    for component in range(3):
        field = velocity[component]
        along_x, across_x = periodic(field, 0, LENGTH_SPACING)
        along_z, across_z = periodic(field, 2, SPAN_SPACING)
        stacked = jnp.einsum('ky,xyz->xkz', operators, field, precision=lax.Precision.HIGHEST)
        wall_first = stacked[:, :NY]
        wall_second = stacked[:, NY:]
        wall_term = VISCOSITY * wall_second - velocity[1] * wall_first
        plane_term = VISCOSITY * (across_x + across_z) - velocity[0] * along_x - velocity[2] * along_z
        tendency = plane_term + wall_term
        results.append(field + TIME_STEP * (GAMMA_NOW * tendency + ZETA_PAST * previous[component]))
    return jnp.stack(results)
```

```python
import functools

import jax
import jax.numpy as jnp
import numpy as np
from jax import lax
from jax.experimental import pallas as pl
from jax.experimental.pallas import tpu as pltpu
from jax.sharding import PartitionSpec as P

NY = 1024


LENGTH_SPACING = 8.0 * 3.141592653589793 / 4096.0
SPAN_SPACING = 3.0 * 3.141592653589793 / 3072.0
VISCOSITY = 1.0 / 2000.0
TIME_STEP = 0.003
GAMMA_NOW = 5.0 / 12.0
ZETA_PAST = -17.0 / 60.0

SCALE = TIME_STEP * GAMMA_NOW
X_FIRST = SCALE / (12.0 * LENGTH_SPACING)
X_SECOND = SCALE * VISCOSITY / (12.0 * LENGTH_SPACING * LENGTH_SPACING)
Z_FIRST = SCALE / (12.0 * SPAN_SPACING)
Z_SECOND = SCALE * VISCOSITY / (12.0 * SPAN_SPACING * SPAN_SPACING)
PAST = TIME_STEP * ZETA_PAST

VMEM_LIMIT = 48 * 1024 * 1024


def chebyshev_matrices(total):
    one = np.float32(1.0)
    ids = np.arange(total, dtype=np.int32)
    angle = np.float32(np.pi) * ids.astype(np.float32) / np.float32(total - 1)
    on_diagonal = ids[:, None] == ids[None, :]
    signs = one - np.float32(2.0) * ((ids[:, None] + ids[None, :]) % 2).astype(np.float32)
    half = np.where((ids == 0) | (ids == total - 1), 0.5, 1.0).astype(np.float32)
    weight_ratio = signs * half[None, :] / half[:, None]
    spacing = (
        np.float32(-2.0)
        * np.sin(np.float32(0.5) * (angle[:, None] + angle[None, :]))
        * np.sin(np.float32(0.5) * (angle[:, None] - angle[None, :]))
    )
    spacing = np.where(on_diagonal, one, spacing)
    first = np.where(on_diagonal, np.float32(0.0), weight_ratio / spacing)
    first_diag = -np.sum(first, axis=1, dtype=np.float32)
    second = np.where(
        on_diagonal,
        np.float32(0.0),
        np.float32(2.0) * first * (first_diag[:, None] - one / spacing),
    )
    second_diag = -np.sum(second, axis=1, dtype=np.float32)
    first[ids, ids] = first_diag
    second[ids, ids] = second_diag
    return first, second


def operator_blocks(total, parts):
    first, second = chebyshev_matrices(total)
    rows = total // parts
    stacked = np.stack(
        [first.astype(np.float64) * SCALE, second.astype(np.float64) * (SCALE * VISCOSITY)]
    ).astype(np.float32)
    blocks = stacked.reshape(2, parts, rows, parts, rows).transpose(1, 3, 0, 2, 4)
    blocks = blocks.reshape(parts, parts, 2 * rows, rows)
    high = blocks.astype(jnp.bfloat16)
    low = (blocks - high.astype(np.float32)).astype(jnp.bfloat16)
    return np.stack([high, low], axis=2)


def wall(operators, fields, v):
    rows = v.shape[1]
    side = jnp.concatenate([fields[0], fields[1]], axis=1)
    high = side.astype(jnp.bfloat16)
    low = (side - high.astype(jnp.float32)).astype(jnp.bfloat16)
    dot = functools.partial(jnp.dot, preferred_element_type=jnp.float32)
    product = dot(operators[0, 0, 0], high) + (
        dot(operators[0, 0, 1], high) + dot(operators[0, 0, 0], low)
    )
    first, second = product[:rows], product[rows:]
    return second - jnp.concatenate([v[0], v[1]], axis=1) * first


def local_kernel(where, operators, velocity, previous, out):
    q = pl.program_id(0)
    field = velocity[pl.ds(q, 1)][0]
    width = field.shape[2]
    added = wall(operators, field, velocity[1])
    parity = where[2]
    along = jnp.where(parity == 0, X_FIRST, -X_FIRST).astype(jnp.float32)
    roll = lambda f, k: pltpu.roll(f, k % width, 1)
    for plane in range(2):
        f, other = field[plane], field[1 - plane]
        u, w = velocity[0, plane], velocity[2, plane]
        step = X_FIRST if plane == 0 else -X_FIRST
        total = X_SECOND * (16.0 * other - 30.0 * f) - u * ((8.0 * step) * other)
        p1, m1, p2, m2 = roll(f, -1), roll(f, 1), roll(f, -2), roll(f, 2)
        total += Z_SECOND * (16.0 * (p1 + m1) - (p2 + m2) - 30.0 * f)
        total -= w * (Z_FIRST * (8.0 * (p1 - m1) - (p2 - m2)))
        total += added[:, plane * width : (plane + 1) * width]
        out[0, plane] = f + PAST * previous[0, plane] + total


def near_kernel(where, velocity, near, base, out):
    parity = where[2]
    inner, outer = 1 - parity, parity
    along = jnp.where(parity == 0, X_FIRST, -X_FIRST).astype(jnp.float32)
    first, second = near[0, parity], near[0, 1 - parity]
    out[0, outer] = base[0, outer] - X_SECOND * first + (along * velocity[0, outer]) * first
    out[0, inner] = (
        base[0, inner]
        + X_SECOND * (16.0 * first - second)
        - (along * velocity[0, inner]) * (8.0 * first - second)
    )


def far_kernel(where, velocity, far, base, out):
    parity = where[2]
    inner, outer = 1 - parity, parity
    along = jnp.where(parity == 0, X_FIRST, -X_FIRST).astype(jnp.float32)
    first, second = far[0, 1 - parity], far[0, parity]
    out[0, inner] = base[0, inner] - X_SECOND * first - (along * velocity[0, inner]) * first
    out[0, outer] = (
        base[0, outer]
        + X_SECOND * (16.0 * first - second)
        + (along * velocity[0, outer]) * (8.0 * first - second)
    )


def remote_kernel(where, operators, velocity, others, base, out):
    added = wall(operators, others[0], velocity[0])
    width = others.shape[3]
    for plane in range(2):
        out[0, plane] = base[0, plane] + added[:, plane * width : (plane + 1) * width]


def call(kernel, where, ins, specs, shape, flops, name):
    one = pl.BlockSpec((1,) + shape[1:], lambda q, where: (q, 0, 0, 0))
    size = int(np.prod(shape)) * 4
    return pl.pallas_call(
        kernel,
        grid_spec=pltpu.PrefetchScalarGridSpec(
            num_scalar_prefetch=1,
            grid=(shape[0],),
            in_specs=specs,
            out_specs=one,
        ),
        out_shape=jax.ShapeDtypeStruct(shape, jnp.float32),
        compiler_params=pltpu.CompilerParams(vmem_limit_bytes=VMEM_LIMIT),
        cost_estimate=pl.CostEstimate(flops=flops, bytes_accessed=4 * size, transcendentals=0),
        name=name,
    )(where, *ins)


def shards(parts, velocity, previous):
    count = lax.axis_size("gx")
    shape = velocity.shape
    assert shape[1] == 2 and count % 2 == 0
    rows = shape[2]
    me = lax.axis_index("gy")
    parity = lax.axis_index("gx") % 2

    outward = [(i, (i - 1) % count if i % 2 == 0 else (i + 1) % count) for i in range(count)]
    inward = [(i, i ^ 1) for i in range(count)]
    others = [
        lax.ppermute(velocity, "gy", [(i, (i + k) % parts) for i in range(parts)])
        for k in range(1, parts)
    ]
    far = lax.ppermute(velocity, "gx", outward)
    near = lax.ppermute(velocity, "gx", inward)

    blocks = jnp.asarray(operator_blocks(rows * parts, parts))

    def where(k):
        return jnp.stack([me, (me - k) % parts, parity]).astype(jnp.int32)

    one = pl.BlockSpec((1,) + shape[1:], lambda q, where: (q, 0, 0, 0))
    whole = pl.BlockSpec(shape, lambda q, where: (0, 0, 0, 0))
    u_only = pl.BlockSpec((1,) + shape[1:], lambda q, where: (0, 0, 0, 0))
    v_only = pl.BlockSpec((1,) + shape[1:], lambda q, where: (1, 0, 0, 0))
    block = pl.BlockSpec(
        (1, 1) + blocks.shape[2:], lambda q, where: (where[0], where[1], 0, 0, 0)
    )
    flops = 2 * 3 * 2 * rows * rows * 6 * shape[3]
    light = 20 * 6 * rows * shape[3]

    total = call(
        local_kernel, where(0), (blocks, velocity, previous), [block, whole, one], shape, flops, "local"
    )
    total = call(near_kernel, where(0), (velocity, near, total), [u_only, one, one], shape, light, "near")
    for k in range(1, parts):
        total = call(
            remote_kernel,
            where(k),
            (blocks, velocity, others[k - 1], total),
            [block, v_only, one, one],
            shape,
            flops,
            "remote",
        )
    return call(far_kernel, where(0), (velocity, far, total), [u_only, one, one], shape, light, "far")


def solution(mesh):
    spec = P(None, "gx", "gy", None)
    body = functools.partial(shards, mesh.shape["gy"])
    return jax.shard_map(body, mesh=mesh, in_specs=(spec, spec), out_specs=spec, check_vma=False)
```

```python
import functools

import jax
import jax.numpy as jnp
import numpy as np
from jax import lax
from jax.experimental import pallas as pl
from jax.experimental.pallas import tpu as pltpu
from jax.sharding import PartitionSpec as P

NY = 1024


LENGTH_SPACING = 8.0 * 3.141592653589793 / 4096.0
SPAN_SPACING = 3.0 * 3.141592653589793 / 3072.0
VISCOSITY = 1.0 / 2000.0
TIME_STEP = 0.003
GAMMA_NOW = 5.0 / 12.0
ZETA_PAST = -17.0 / 60.0

SCALE = TIME_STEP * GAMMA_NOW
X_FIRST = SCALE / (12.0 * LENGTH_SPACING)
X_SECOND = SCALE * VISCOSITY / (12.0 * LENGTH_SPACING * LENGTH_SPACING)
Z_FIRST = SCALE / (12.0 * SPAN_SPACING)
Z_SECOND = SCALE * VISCOSITY / (12.0 * SPAN_SPACING * SPAN_SPACING)
PAST = TIME_STEP * ZETA_PAST

VMEM_LIMIT = 24 * 1024 * 1024


def chebyshev_matrices(total):
    one = np.float32(1.0)
    ids = np.arange(total, dtype=np.int32)
    angle = ids.astype(np.float32) * (np.float32(np.pi) / np.float32(total - 1))
    on_diagonal = ids[:, None] == ids[None, :]
    signs = one - np.float32(2.0) * ((ids[:, None] + ids[None, :]) % 2).astype(np.float32)
    half = np.where((ids == 0) | (ids == total - 1), 0.5, 1.0).astype(np.float32)
    weight_ratio = signs * half[None, :] / half[:, None]
    spacing = (
        np.float32(-2.0)
        * np.sin(np.float32(0.5) * (angle[:, None] + angle[None, :]))
        * np.sin(np.float32(0.5) * (angle[:, None] - angle[None, :]))
    )
    spacing = np.where(on_diagonal, one, spacing)
    first = np.where(on_diagonal, np.float32(0.0), weight_ratio / spacing)
    first_diag = -np.sum(first, axis=1, dtype=np.float32)
    second = np.where(
        on_diagonal,
        np.float32(0.0),
        np.float32(2.0) * first * (first_diag[:, None] - one / spacing),
    )
    second_diag = -np.sum(second, axis=1, dtype=np.float32)
    first[ids, ids] = first_diag
    second[ids, ids] = second_diag
    return first, second


def operator_blocks(total, parts):
    first, second = chebyshev_matrices(total)
    rows = total // parts
    stacked = np.stack(
        [first.astype(np.float64) * SCALE, second.astype(np.float64) * (SCALE * VISCOSITY)]
    ).astype(np.float32)
    blocks = stacked.reshape(2, parts, rows, parts, rows).transpose(1, 3, 0, 2, 4)
    blocks = blocks.reshape(parts, parts, 2 * rows, rows)
    high = blocks.astype(jnp.bfloat16)
    low = (blocks - high.astype(np.float32)).astype(jnp.bfloat16)
    return np.stack([high, low], axis=2)


def wall(operators, fields, v):
    rows = v.shape[1]
    side = jnp.concatenate([fields[0], fields[1]], axis=1)
    high = side.astype(jnp.bfloat16)
    low = (side - high.astype(jnp.float32)).astype(jnp.bfloat16)
    dot = functools.partial(jnp.dot, preferred_element_type=jnp.float32)
    product = dot(operators[0], high) + (dot(operators[1], high) + dot(operators[0], low))
    first, second = product[:rows], product[rows:]
    added = second - jnp.concatenate([v[0], v[1]], axis=1) * first
    return added[:, : v.shape[2]], added[:, v.shape[2] :]


def along_x(parity):
    return jnp.where(parity == 0, X_FIRST, -X_FIRST).astype(jnp.float32)


def local_kernel(operators, velocity, previous, *outs):
    width = velocity.shape[3]
    roll = lambda f, k: pltpu.roll(f, k % width, 1)
    for q in range(3):
        added = wall(operators, velocity[q], velocity[1])
        for plane in range(2):
            f, other = velocity[q, plane], velocity[q, 1 - plane]
            u, w = velocity[0, plane], velocity[2, plane]
            step = X_FIRST if plane == 0 else -X_FIRST
            total = X_SECOND * (16.0 * other - 30.0 * f) - u * ((8.0 * step) * other)
            p1, m1, p2, m2 = roll(f, -1), roll(f, 1), roll(f, -2), roll(f, 2)
            total += Z_SECOND * (16.0 * (p1 + m1) - (p2 + m2) - 30.0 * f)
            total -= w * (Z_FIRST * (8.0 * (p1 - m1) - (p2 - m2)))
            outs[q][plane] = f + PAST * previous[q, plane] + (total + added[plane])


def near_kernel(where, velocity, near, *refs):
    bases, outs, (slab, came) = refs[:3], refs[3:6], refs[6:]
    parity = where[0]
    inner, outer = 1 - parity, parity
    along = along_x(parity)
    fetches = [pltpu.make_async_copy(near.at[q], slab.at[q], came.at[q]) for q in range(3)]
    for fetch in fetches:
        fetch.start()
    for q in range(3):
        fetches[q].wait()
        base, out = bases[q], outs[q]
        first, second = slab[q, parity], slab[q, 1 - parity]
        out[outer] = base[outer] - X_SECOND * first + (along * velocity[0, outer]) * first
        out[inner] = (
            base[inner]
            + X_SECOND * (16.0 * first - second)
            - (along * velocity[0, inner]) * (8.0 * first - second)
        )


def remote_kernel(operators, velocity, others, *refs):
    for q in range(3):
        base, out = refs[q], refs[3 + q]
        added = wall(operators, others[q], velocity[1])
        for plane in range(2):
            out[plane] = base[plane] + added[plane]


def far_kernel(where, velocity, far, *refs):
    bases, (out, total, sent) = refs[:3], refs[3:]
    parity = where[0]
    inner, outer = 1 - parity, parity
    along = along_x(parity)
    stores = []
    for q in range(3):
        first, second = far[q, 1 - parity], far[q, parity]
        total[q, inner] = (
            bases[q][inner] - X_SECOND * first - (along * velocity[0, inner]) * first
        )
        total[q, outer] = (
            bases[q][outer]
            + X_SECOND * (16.0 * first - second)
            + (along * velocity[0, outer]) * (8.0 * first - second)
        )
        stores.append(pltpu.make_async_copy(total.at[q], out.at[q], sent.at[q]))
        stores[-1].start()
    for store in stores:
        store.wait()


VMEM = pl.BlockSpec(memory_space=pltpu.VMEM)
SMEM = pl.BlockSpec(memory_space=pltpu.SMEM)
ANY = pl.BlockSpec(memory_space=pl.ANY)


def vmem(array):
    return pltpu.with_memory_space_constraint(array, pltpu.VMEM)


def call(kernel, ins, in_specs, out_shape, flops, name, **kwargs):
    leaves = jax.tree.leaves(out_shape)
    kwargs.setdefault("out_specs", jax.tree.map(lambda _: VMEM, out_shape))
    size = sum(int(np.prod(x.shape)) * x.dtype.itemsize for x in (*ins, *leaves))
    return pl.pallas_call(
        kernel,
        in_specs=in_specs,
        out_shape=out_shape,
        compiler_params=pltpu.CompilerParams(vmem_limit_bytes=VMEM_LIMIT),
        cost_estimate=pl.CostEstimate(flops=flops, bytes_accessed=size, transcendentals=0),
        name=name,
        **kwargs,
    )(*ins)


def shards(parts, velocity, previous):
    count = lax.axis_size("gx")
    shape = velocity.shape
    assert shape[0] == 3 and shape[1] == 2 and count % 2 == 0
    rows = shape[2]
    me = lax.axis_index("gy")
    parity = (lax.axis_index("gx") % 2).astype(jnp.int32).reshape(1)

    outward = [(i, (i - 1) % count if i % 2 == 0 else (i + 1) % count) for i in range(count)]
    inward = [(i, i ^ 1) for i in range(count)]
    far = lax.ppermute(velocity, "gx", outward)
    near = lax.ppermute(velocity, "gx", inward)
    others = [
        lax.ppermute(velocity, "gy", [(i, (i + k) % parts) for i in range(parts)])
        for k in range(1, parts)
    ]

    blocks = jnp.asarray(operator_blocks(rows * parts, parts))
    mine = lax.dynamic_index_in_dim(blocks, me, 0, keepdims=False)
    operators = [
        lax.dynamic_index_in_dim(mine, (me - k) % parts, 0, keepdims=False) for k in range(parts)
    ]

    one = jax.ShapeDtypeStruct(shape[1:], jnp.float32)
    whole = jax.ShapeDtypeStruct(shape, jnp.float32)
    flops = 3 * 2 * 2 * 2 * rows * rows * 6 * shape[3]
    light = 20 * 6 * rows * shape[3]
    totals = call(
        local_kernel,
        (operators[0], velocity, previous),
        [VMEM] * 3,
        (one,) * 3,
        flops,
        "local",
    )
    totals = call(
        near_kernel,
        (parity, velocity, pltpu.with_memory_space_constraint(near, pltpu.HBM), *totals),
        [SMEM, VMEM, ANY] + [VMEM] * 3,
        (one,) * 3,
        light,
        "near",
        scratch_shapes=[pltpu.VMEM(shape, jnp.float32), pltpu.SemaphoreType.DMA((3,))],
    )
    for k in range(1, parts):
        totals = call(
            remote_kernel,
            (vmem(operators[k]), vmem(velocity), vmem(others[k - 1]), *totals),
            [VMEM] * 6,
            (one,) * 3,
            flops,
            "remote",
        )
    return call(
        far_kernel,
        (parity, vmem(velocity), vmem(far), *totals),
        [SMEM, VMEM, VMEM] + [VMEM] * 3,
        whole,
        light,
        "far",
        out_specs=ANY,
        scratch_shapes=[
            pltpu.VMEM(shape, jnp.float32),
            pltpu.SemaphoreType.DMA((3,)),
        ],
    )


def solution(mesh):
    spec = P(None, "gx", "gy", None)
    body = functools.partial(shards, mesh.shape["gy"])
    return jax.shard_map(body, mesh=mesh, in_specs=(spec, spec), out_specs=spec, check_vma=False)
```

```python
import functools

import jax
import jax.numpy as jnp
import numpy as np
from jax import lax
from jax.experimental import pallas as pl
from jax.experimental.pallas import tpu as pltpu
from jax.sharding import PartitionSpec as P

NY = 1024


LENGTH_SPACING = 8.0 * 3.141592653589793 / 4096.0
SPAN_SPACING = 3.0 * 3.141592653589793 / 3072.0
VISCOSITY = 1.0 / 2000.0
TIME_STEP = 0.003
GAMMA_NOW = 5.0 / 12.0
ZETA_PAST = -17.0 / 60.0

SCALE = TIME_STEP * GAMMA_NOW
X_FIRST = SCALE / (12.0 * LENGTH_SPACING)
X_SECOND = SCALE * VISCOSITY / (12.0 * LENGTH_SPACING * LENGTH_SPACING)
Z_FIRST = SCALE / (12.0 * SPAN_SPACING)
Z_SECOND = SCALE * VISCOSITY / (12.0 * SPAN_SPACING * SPAN_SPACING)
PAST = TIME_STEP * ZETA_PAST

VMEM_LIMIT = 24 * 1024 * 1024
PIECES = ((0, 1), (2,))


def chebyshev_matrices(total):
    one = np.float32(1.0)
    ids = np.arange(total, dtype=np.int32)
    angle = ids.astype(np.float32) * (np.float32(np.pi) / np.float32(total - 1))
    on_diagonal = ids[:, None] == ids[None, :]
    signs = one - np.float32(2.0) * ((ids[:, None] + ids[None, :]) % 2).astype(np.float32)
    half = np.where((ids == 0) | (ids == total - 1), 0.5, 1.0).astype(np.float32)
    weight_ratio = signs * half[None, :] / half[:, None]
    spacing = (
        np.float32(-2.0)
        * np.sin(np.float32(0.5) * (angle[:, None] + angle[None, :]))
        * np.sin(np.float32(0.5) * (angle[:, None] - angle[None, :]))
    )
    spacing = np.where(on_diagonal, one, spacing)
    first = np.where(on_diagonal, np.float32(0.0), weight_ratio / spacing)
    first_diag = -np.sum(first, axis=1, dtype=np.float32)
    second = np.where(
        on_diagonal,
        np.float32(0.0),
        np.float32(2.0) * first * (first_diag[:, None] - one / spacing),
    )
    second_diag = -np.sum(second, axis=1, dtype=np.float32)
    first[ids, ids] = first_diag
    second[ids, ids] = second_diag
    return first, second


def operator_blocks(total, parts):
    first, second = chebyshev_matrices(total)
    rows = total // parts
    stacked = np.stack(
        [first.astype(np.float64) * SCALE, second.astype(np.float64) * (SCALE * VISCOSITY)]
    ).astype(np.float32)
    blocks = stacked.reshape(2, parts, rows, parts, rows).transpose(1, 3, 0, 2, 4)
    blocks = blocks.reshape(parts, parts, 2 * rows, rows)
    high = blocks.astype(jnp.bfloat16)
    low = (blocks - high.astype(np.float32)).astype(jnp.bfloat16)
    return np.stack([high, low], axis=2)


def wall(operators, fields, v):
    rows = v.shape[1]
    side = jnp.concatenate([fields[0], fields[1]], axis=1)
    high = side.astype(jnp.bfloat16)
    low = (side - high.astype(jnp.float32)).astype(jnp.bfloat16)
    dot = functools.partial(jnp.dot, preferred_element_type=jnp.float32)
    product = dot(operators[0], high) + (dot(operators[1], high) + dot(operators[0], low))
    first, second = product[:rows], product[rows:]
    added = second - jnp.concatenate([v[0], v[1]], axis=1) * first
    return added[:, : v.shape[2]], added[:, v.shape[2] :]


def along_x(parity):
    return jnp.where(parity == 0, X_FIRST, -X_FIRST).astype(jnp.float32)


def local_kernel(blocks, velocity, previous, *refs):
    outs, parted = refs[:3], refs[3 : 3 + len(PIECES)]
    own, past, operators, came, sent = refs[3 + len(PIECES) :]
    me = lax.axis_index("gy")
    fetches = [
        pltpu.make_async_copy(velocity, own, came.at[0]),
        pltpu.make_async_copy(blocks.at[me, me], operators, came.at[1]),
        pltpu.make_async_copy(previous, past, came.at[2]),
    ]
    for fetch in fetches:
        fetch.start()
    fetches[0].wait()
    stores = [
        pltpu.make_async_copy(own.at[c[0] : c[-1] + 1], part, sent.at[i])
        for i, (c, part) in enumerate(zip(PIECES, parted))
    ]
    for store in stores:
        store.start()
    for fetch in fetches[1:]:
        fetch.wait()
    width = own.shape[3]
    roll = lambda f, k: pltpu.roll(f, k % width, 1)
    for q in range(3):
        added = wall(operators, own[q], own[1])
        for plane in range(2):
            f, other = own[q, plane], own[q, 1 - plane]
            u, w = own[0, plane], own[2, plane]
            step = X_FIRST if plane == 0 else -X_FIRST
            total = X_SECOND * (16.0 * other - 30.0 * f) - u * ((8.0 * step) * other)
            p1, m1, p2, m2 = roll(f, -1), roll(f, 1), roll(f, -2), roll(f, 2)
            total += Z_SECOND * (16.0 * (p1 + m1) - (p2 + m2) - 30.0 * f)
            total -= w * (Z_FIRST * (8.0 * (p1 - m1) - (p2 - m2)))
            outs[q][plane] = f + PAST * past[q, plane] + (total + added[plane])
    for store in stores:
        store.wait()


def near_kernel(velocity, *refs):
    near, refs = refs[: len(PIECES)], refs[len(PIECES) :]
    bases, outs, (u, slab, came) = refs[:3], refs[3:6], refs[6:]
    parity = lax.axis_index("gx") % 2
    inner, outer = 1 - parity, parity
    along = along_x(parity)
    fetches = [
        pltpu.make_async_copy(part.at[i], slab.at[q], came.at[q])
        for c, part in zip(PIECES, near)
        for i, q in enumerate(c)
    ]
    fetches.append(pltpu.make_async_copy(velocity.at[0], u, came.at[3]))
    for fetch in fetches:
        fetch.start()
    fetches[3].wait()
    for q in range(3):
        fetches[q].wait()
        base, out = bases[q], outs[q]
        first, second = slab[q, parity], slab[q, 1 - parity]
        out[outer] = base[outer] - X_SECOND * first + (along * u[outer]) * first
        out[inner] = (
            base[inner]
            + X_SECOND * (16.0 * first - second)
            - (along * u[inner]) * (8.0 * first - second)
        )


def remote_kernel(operators, velocity, others, *refs):
    for q in range(3):
        base, out = refs[q], refs[3 + q]
        added = wall(operators, others[q], velocity[1])
        for plane in range(2):
            out[plane] = base[plane] + added[plane]


def far_kernel(velocity, far, *refs):
    bases, (out, total, sent) = refs[:3], refs[3:]
    parity = lax.axis_index("gx") % 2
    inner, outer = 1 - parity, parity
    along = along_x(parity)
    stores = []
    for q in range(3):
        first, second = far[q, 1 - parity], far[q, parity]
        total[q, inner] = (
            bases[q][inner] - X_SECOND * first - (along * velocity[0, inner]) * first
        )
        total[q, outer] = (
            bases[q][outer]
            + X_SECOND * (16.0 * first - second)
            + (along * velocity[0, outer]) * (8.0 * first - second)
        )
        stores.append(pltpu.make_async_copy(total.at[q], out.at[q], sent.at[q]))
        stores[-1].start()
    for store in stores:
        store.wait()


VMEM = pl.BlockSpec(memory_space=pltpu.VMEM)
ANY = pl.BlockSpec(memory_space=pl.ANY)


def vmem(array):
    return pltpu.with_memory_space_constraint(array, pltpu.VMEM)


def hbm(array):
    return pltpu.with_memory_space_constraint(array, pltpu.HBM)


def call(kernel, ins, in_specs, out_shape, name, **kwargs):
    kwargs.setdefault("out_specs", jax.tree.map(lambda _: VMEM, out_shape))
    return pl.pallas_call(
        kernel,
        in_specs=in_specs,
        out_shape=out_shape,
        compiler_params=pltpu.CompilerParams(vmem_limit_bytes=VMEM_LIMIT),
        cost_estimate=pl.CostEstimate(flops=0, bytes_accessed=0, transcendentals=0),
        name=name,
        **kwargs,
    )(*ins)


def shards(parts, velocity, previous):
    count = lax.axis_size("gx")
    shape = velocity.shape
    assert shape[0] == 3 and shape[1] == 2 and count % 2 == 0
    rows = shape[2]
    me = lax.axis_index("gy")

    outward = [(i, (i - 1) % count if i % 2 == 0 else (i + 1) % count) for i in range(count)]
    inward = [(i, i ^ 1) for i in range(count)]
    far = lax.ppermute(velocity, "gx", outward)
    others = [
        lax.ppermute(velocity, "gy", [(i, (i + k) % parts) for i in range(parts)])
        for k in range(1, parts)
    ]

    blocks = jnp.asarray(operator_blocks(rows * parts, parts))
    mine = lax.dynamic_index_in_dim(blocks, me, 0, keepdims=False)
    operators = [
        lax.dynamic_index_in_dim(mine, (me - k) % parts, 0, keepdims=False)
        for k in range(1, parts)
    ]

    one = jax.ShapeDtypeStruct(shape[1:], jnp.float32)
    whole = jax.ShapeDtypeStruct(shape, jnp.float32)
    totals = call(
        local_kernel,
        (hbm(blocks), hbm(velocity), hbm(previous)),
        [ANY] * 3,
        (one,) * 3
        + tuple(jax.ShapeDtypeStruct((len(c),) + shape[1:], jnp.float32) for c in PIECES),
        "local",
        out_specs=(VMEM,) * 3 + (ANY,) * len(PIECES),
        scratch_shapes=[
            pltpu.VMEM(shape, jnp.float32),
            pltpu.VMEM(shape, jnp.float32),
            pltpu.VMEM(blocks.shape[2:], jnp.bfloat16),
            pltpu.SemaphoreType.DMA((3,)),
            pltpu.SemaphoreType.DMA((len(PIECES),)),
        ],
    )
    near = [lax.ppermute(part, "gx", inward) for part in totals[3:]]
    totals = call(
        near_kernel,
        (hbm(velocity), *map(hbm, near), *totals[:3]),
        [ANY] * (1 + len(PIECES)) + [VMEM] * 3,
        (one,) * 3,
        "near",
        scratch_shapes=[
            pltpu.VMEM(shape[1:], jnp.float32),
            pltpu.VMEM(shape, jnp.float32),
            pltpu.SemaphoreType.DMA((4,)),
        ],
    )
    for k in range(1, parts):
        totals = call(
            remote_kernel,
            (vmem(operators[k - 1]), vmem(velocity), vmem(others[k - 1]), *totals),
            [VMEM] * 6,
            (one,) * 3,
            "remote",
        )
    return call(
        far_kernel,
        (vmem(velocity), vmem(far), *totals),
        [VMEM] * 5,
        whole,
        "far",
        out_specs=ANY,
        scratch_shapes=[
            pltpu.VMEM(shape, jnp.float32),
            pltpu.SemaphoreType.DMA((3,)),
        ],
    )


def solution(mesh):
    spec = P(None, "gx", "gy", None)
    body = functools.partial(shards, mesh.shape["gy"])
    return jax.shard_map(body, mesh=mesh, in_specs=(spec, spec), out_specs=spec, check_vma=False)
```

```python
import functools

import jax
import jax.numpy as jnp
import numpy as np
from jax import lax
from jax.experimental import pallas as pl
from jax.experimental.pallas import tpu as pltpu
from jax.sharding import PartitionSpec as P

NY = 1024


LENGTH_SPACING = 8.0 * 3.141592653589793 / 4096.0
SPAN_SPACING = 3.0 * 3.141592653589793 / 3072.0
VISCOSITY = 1.0 / 2000.0
TIME_STEP = 0.003
GAMMA_NOW = 5.0 / 12.0
ZETA_PAST = -17.0 / 60.0

SCALE = TIME_STEP * GAMMA_NOW
X_FIRST = SCALE / (12.0 * LENGTH_SPACING)
X_SECOND = SCALE * VISCOSITY / (12.0 * LENGTH_SPACING * LENGTH_SPACING)
Z_FIRST = SCALE / (12.0 * SPAN_SPACING)
Z_SECOND = SCALE * VISCOSITY / (12.0 * SPAN_SPACING * SPAN_SPACING)
PAST = TIME_STEP * ZETA_PAST

VMEM_LIMIT = 24 * 1024 * 1024
PIECES = ((0, 1), (2,))
COARSE_LARGEST = 224.0
COARSE_LIFT = 32.0
LOW_LIFT = 512.0


def chebyshev_matrices(total):
    one = np.float32(1.0)
    ids = np.arange(total, dtype=np.int32)
    angle = ids.astype(np.float32) * (np.float32(np.pi) / np.float32(total - 1))
    on_diagonal = ids[:, None] == ids[None, :]
    signs = one - np.float32(2.0) * ((ids[:, None] + ids[None, :]) % 2).astype(np.float32)
    half = np.where((ids == 0) | (ids == total - 1), 0.5, 1.0).astype(np.float32)
    weight_ratio = signs * half[None, :] / half[:, None]
    spacing = (
        np.float32(-2.0)
        * np.sin(np.float32(0.5) * (angle[:, None] + angle[None, :]))
        * np.sin(np.float32(0.5) * (angle[:, None] - angle[None, :]))
    )
    spacing = np.where(on_diagonal, one, spacing)
    first = np.where(on_diagonal, np.float32(0.0), weight_ratio / spacing)
    first_diag = -np.sum(first, axis=1, dtype=np.float32)
    second = np.where(
        on_diagonal,
        np.float32(0.0),
        np.float32(2.0) * first * (first_diag[:, None] - one / spacing),
    )
    second_diag = -np.sum(second, axis=1, dtype=np.float32)
    first[ids, ids] = first_diag
    second[ids, ids] = second_diag
    return first, second


def operator_blocks(total, parts):
    first, second = chebyshev_matrices(total)
    rows = total // parts
    stacked = np.stack(
        [first.astype(np.float64) * SCALE, second.astype(np.float64) * (SCALE * VISCOSITY)]
    ).astype(np.float32)
    blocks = stacked.reshape(2, parts, rows, parts, rows).transpose(1, 3, 0, 2, 4)
    mine = np.arange(parts)
    own = blocks[mine, mine]
    there = np.stack([blocks[mine, (mine - k) % parts] for k in range(1, parts)], axis=1)
    largest = np.max(np.abs(there), axis=(0, 1, 3, 4))
    scale = np.exp2(np.floor(np.log2(COARSE_LARGEST / largest))).astype(np.float32)
    own = own.reshape(parts, 2 * rows, rows)
    high = own.astype(jnp.bfloat16)
    own = np.stack([high, (own - high.astype(np.float32)).astype(jnp.bfloat16)], axis=1)
    high = there.astype(jnp.bfloat16)
    low = there - high.astype(np.float32)
    coarse = np.concatenate([LOW_LIFT * low, there], axis=-1) * scale[:, None, None]
    coarse = coarse.astype(jnp.float8_e4m3fn)
    shape = (parts, parts - 1, 2 * rows)
    undo = [float(1.0 / (x * LOW_LIFT * COARSE_LIFT)) for x in scale]
    return own, high.reshape(shape + (rows,)), coarse.reshape(shape + (2 * rows,)), undo


def wall(operators, fields, v):
    rows = v.shape[1]
    side = jnp.concatenate([fields[0], fields[1]], axis=1)
    high = side.astype(jnp.bfloat16)
    low = (side - high.astype(jnp.float32)).astype(jnp.bfloat16)
    dot = functools.partial(jnp.dot, preferred_element_type=jnp.float32)
    product = dot(operators[0], high) + (dot(operators[1], high) + dot(operators[0], low))
    first, second = product[:rows], product[rows:]
    added = second - jnp.concatenate([v[0], v[1]], axis=1) * first
    return added[:, : v.shape[2]], added[:, v.shape[2] :]


def wall_there(undo, high_operators, coarse_operators, fields, v):
    rows = v.shape[1]
    side = jnp.concatenate([fields[0], fields[1]], axis=1)
    high = side.astype(jnp.bfloat16)
    low = side - high.astype(jnp.float32)
    coarse = jnp.concatenate(
        [
            (COARSE_LIFT * side).astype(jnp.float8_e4m3fn),
            (LOW_LIFT * COARSE_LIFT * low).astype(jnp.float8_e4m3fn),
        ],
        axis=0,
    )
    dot = functools.partial(jnp.dot, preferred_element_type=jnp.float32)
    product = dot(high_operators[...], high)
    rest = dot(coarse_operators[...], coarse)
    first = product[:rows] + undo[0] * rest[:rows]
    second = product[rows:] + undo[1] * rest[rows:]
    added = second - jnp.concatenate([v[0], v[1]], axis=1) * first
    return added[:, : v.shape[2]], added[:, v.shape[2] :]


def along_x(parity):
    return jnp.where(parity == 0, X_FIRST, -X_FIRST).astype(jnp.float32)


def local_kernel(blocks, velocity, previous, *refs):
    outs, parted = refs[:3], refs[3 : 3 + len(PIECES)]
    own, past, operators, came, sent = refs[3 + len(PIECES) :]
    me = lax.axis_index("gy")
    fetches = [
        pltpu.make_async_copy(velocity, own, came.at[0]),
        pltpu.make_async_copy(blocks.at[me], operators, came.at[1]),
        pltpu.make_async_copy(previous, past, came.at[2]),
    ]
    for fetch in fetches:
        fetch.start()
    fetches[0].wait()
    stores = [
        pltpu.make_async_copy(own.at[c[0] : c[-1] + 1], part, sent.at[i])
        for i, (c, part) in enumerate(zip(PIECES, parted))
    ]
    for store in stores:
        store.start()
    for fetch in fetches[1:]:
        fetch.wait()
    width = own.shape[3]
    roll = lambda f, k: pltpu.roll(f, k % width, 1)
    for q in range(3):
        added = wall(operators, own[q], own[1])
        for plane in range(2):
            f, other = own[q, plane], own[q, 1 - plane]
            u, w = own[0, plane], own[2, plane]
            step = X_FIRST if plane == 0 else -X_FIRST
            total = X_SECOND * (16.0 * other - 30.0 * f) - u * ((8.0 * step) * other)
            p1, m1, p2, m2 = roll(f, -1), roll(f, 1), roll(f, -2), roll(f, 2)
            total += Z_SECOND * (16.0 * (p1 + m1) - (p2 + m2) - 30.0 * f)
            total -= w * (Z_FIRST * (8.0 * (p1 - m1) - (p2 - m2)))
            outs[q][plane] = f + PAST * past[q, plane] + (total + added[plane])
    for store in stores:
        store.wait()


def near_kernel(velocity, *refs):
    near, refs = refs[: len(PIECES)], refs[len(PIECES) :]
    bases, outs, (u, slab, came) = refs[:3], refs[3:6], refs[6:]
    parity = lax.axis_index("gx") % 2
    inner, outer = 1 - parity, parity
    along = along_x(parity)
    fetches = [
        pltpu.make_async_copy(part.at[i], slab.at[q], came.at[q])
        for c, part in zip(PIECES, near)
        for i, q in enumerate(c)
    ]
    fetches.append(pltpu.make_async_copy(velocity.at[0], u, came.at[3]))
    for fetch in fetches:
        fetch.start()
    fetches[3].wait()
    for q in range(3):
        fetches[q].wait()
        base, out = bases[q], outs[q]
        first, second = slab[q, parity], slab[q, 1 - parity]
        out[outer] = base[outer] - X_SECOND * first + (along * u[outer]) * first
        out[inner] = (
            base[inner]
            + X_SECOND * (16.0 * first - second)
            - (along * u[inner]) * (8.0 * first - second)
        )


def remote_kernel(undo, high_operators, coarse_operators, velocity, others, *refs):
    for q in range(3):
        base, out = refs[q], refs[3 + q]
        added = wall_there(undo, high_operators, coarse_operators, others[q], velocity[1])
        for plane in range(2):
            out[plane] = base[plane] + added[plane]


def far_kernel(velocity, far, *refs):
    bases, (out, total, sent) = refs[:3], refs[3:]
    parity = lax.axis_index("gx") % 2
    inner, outer = 1 - parity, parity
    along = along_x(parity)
    stores = []
    for q in range(3):
        first, second = far[q, 1 - parity], far[q, parity]
        total[q, inner] = (
            bases[q][inner] - X_SECOND * first - (along * velocity[0, inner]) * first
        )
        total[q, outer] = (
            bases[q][outer]
            + X_SECOND * (16.0 * first - second)
            + (along * velocity[0, outer]) * (8.0 * first - second)
        )
        stores.append(pltpu.make_async_copy(total.at[q], out.at[q], sent.at[q]))
        stores[-1].start()
    for store in stores:
        store.wait()


VMEM = pl.BlockSpec(memory_space=pltpu.VMEM)
ANY = pl.BlockSpec(memory_space=pl.ANY)


def vmem(array):
    return pltpu.with_memory_space_constraint(array, pltpu.VMEM)


def hbm(array):
    return pltpu.with_memory_space_constraint(array, pltpu.HBM)


def call(kernel, ins, in_specs, out_shape, name, **kwargs):
    kwargs.setdefault("out_specs", jax.tree.map(lambda _: VMEM, out_shape))
    return pl.pallas_call(
        kernel,
        in_specs=in_specs,
        out_shape=out_shape,
        compiler_params=pltpu.CompilerParams(vmem_limit_bytes=VMEM_LIMIT),
        cost_estimate=pl.CostEstimate(flops=0, bytes_accessed=0, transcendentals=0),
        name=name,
        **kwargs,
    )(*ins)


def shards(parts, velocity, previous):
    count = lax.axis_size("gx")
    shape = velocity.shape
    assert shape[0] == 3 and shape[1] == 2 and count % 2 == 0
    rows = shape[2]
    me = lax.axis_index("gy")

    outward = [(i, (i - 1) % count if i % 2 == 0 else (i + 1) % count) for i in range(count)]
    inward = [(i, i ^ 1) for i in range(count)]
    far = lax.ppermute(velocity, "gx", outward)
    others = [
        lax.ppermute(velocity, "gy", [(i, (i + k) % parts) for i in range(parts)])
        for k in range(1, parts)
    ]

    own, high, coarse, undo = operator_blocks(rows * parts, parts)
    own = jnp.asarray(own)
    high = lax.dynamic_index_in_dim(jnp.asarray(high), me, 0, keepdims=False)
    coarse = lax.dynamic_index_in_dim(jnp.asarray(coarse), me, 0, keepdims=False)

    one = jax.ShapeDtypeStruct(shape[1:], jnp.float32)
    whole = jax.ShapeDtypeStruct(shape, jnp.float32)
    totals = call(
        local_kernel,
        (hbm(own), hbm(velocity), hbm(previous)),
        [ANY] * 3,
        (one,) * 3
        + tuple(jax.ShapeDtypeStruct((len(c),) + shape[1:], jnp.float32) for c in PIECES),
        "local",
        out_specs=(VMEM,) * 3 + (ANY,) * len(PIECES),
        scratch_shapes=[
            pltpu.VMEM(shape, jnp.float32),
            pltpu.VMEM(shape, jnp.float32),
            pltpu.VMEM(own.shape[1:], jnp.bfloat16),
            pltpu.SemaphoreType.DMA((3,)),
            pltpu.SemaphoreType.DMA((len(PIECES),)),
        ],
    )
    near = [lax.ppermute(part, "gx", inward) for part in totals[3:]]
    totals = call(
        near_kernel,
        (hbm(velocity), *map(hbm, near), *totals[:3]),
        [ANY] * (1 + len(PIECES)) + [VMEM] * 3,
        (one,) * 3,
        "near",
        scratch_shapes=[
            pltpu.VMEM(shape[1:], jnp.float32),
            pltpu.VMEM(shape, jnp.float32),
            pltpu.SemaphoreType.DMA((4,)),
        ],
    )
    for k in range(1, parts):
        totals = call(
            functools.partial(remote_kernel, undo),
            (
                *map(vmem, (high[k - 1], coarse[k - 1], velocity, others[k - 1])),
                *totals,
            ),
            [VMEM] * 7,
            (one,) * 3,
            "remote",
        )
    return call(
        far_kernel,
        (vmem(velocity), vmem(far), *totals),
        [VMEM] * 5,
        whole,
        "far",
        out_specs=ANY,
        scratch_shapes=[
            pltpu.VMEM(shape, jnp.float32),
            pltpu.SemaphoreType.DMA((3,)),
        ],
    )


def solution(mesh):
    spec = P(None, "gx", "gy", None)
    body = functools.partial(shards, mesh.shape["gy"])
    return jax.shard_map(body, mesh=mesh, in_specs=(spec, spec), out_specs=spec, check_vma=False)
```

```python
import functools

import jax
import jax.numpy as jnp
import numpy as np
from jax import lax
from jax.experimental import pallas as pl
from jax.experimental.pallas import tpu as pltpu
from jax.sharding import PartitionSpec as P

NY = 1024


LENGTH_SPACING = 8.0 * 3.141592653589793 / 4096.0
SPAN_SPACING = 3.0 * 3.141592653589793 / 3072.0
VISCOSITY = 1.0 / 2000.0
TIME_STEP = 0.003
GAMMA_NOW = 5.0 / 12.0
ZETA_PAST = -17.0 / 60.0

SCALE = TIME_STEP * GAMMA_NOW
X_FIRST = SCALE / (12.0 * LENGTH_SPACING)
X_SECOND = SCALE * VISCOSITY / (12.0 * LENGTH_SPACING * LENGTH_SPACING)
Z_FIRST = SCALE / (12.0 * SPAN_SPACING)
Z_SECOND = SCALE * VISCOSITY / (12.0 * SPAN_SPACING * SPAN_SPACING)
PAST = TIME_STEP * ZETA_PAST

VMEM_LIMIT = 24 * 1024 * 1024
PIECES = ((0, 1), (2,))
COARSE_LARGEST = 224.0
COARSE_LIFT = 32.0
LOW_LIFT = 512.0


def chebyshev_matrices(total):
    one = np.float32(1.0)
    ids = np.arange(total, dtype=np.int32)
    angle = ids.astype(np.float32) * (np.float32(np.pi) / np.float32(total - 1))
    on_diagonal = ids[:, None] == ids[None, :]
    signs = one - np.float32(2.0) * ((ids[:, None] + ids[None, :]) % 2).astype(np.float32)
    half = np.where((ids == 0) | (ids == total - 1), 0.5, 1.0).astype(np.float32)
    weight_ratio = signs * half[None, :] / half[:, None]
    spacing = (
        np.float32(-2.0)
        * np.sin(np.float32(0.5) * (angle[:, None] + angle[None, :]))
        * np.sin(np.float32(0.5) * (angle[:, None] - angle[None, :]))
    )
    spacing = np.where(on_diagonal, one, spacing)
    first = np.where(on_diagonal, np.float32(0.0), weight_ratio / spacing)
    first_diag = -np.sum(first, axis=1, dtype=np.float32)
    second = np.where(
        on_diagonal,
        np.float32(0.0),
        np.float32(2.0) * first * (first_diag[:, None] - one / spacing),
    )
    second_diag = -np.sum(second, axis=1, dtype=np.float32)
    first[ids, ids] = first_diag
    second[ids, ids] = second_diag
    return first, second


def operator_blocks(total, parts):
    first, second = chebyshev_matrices(total)
    rows = total // parts
    stacked = np.stack(
        [first.astype(np.float64) * SCALE, second.astype(np.float64) * (SCALE * VISCOSITY)]
    ).astype(np.float32)
    blocks = stacked.reshape(2, parts, rows, parts, rows).transpose(1, 3, 0, 2, 4)
    mine = np.arange(parts)
    own = blocks[mine, mine]
    there = np.stack([blocks[mine, (mine - k) % parts] for k in range(1, parts)], axis=1)
    largest = np.max(np.abs(there), axis=(0, 1, 3, 4))
    scale = np.exp2(np.floor(np.log2(COARSE_LARGEST / largest))).astype(np.float32)
    own = own.reshape(parts, 2 * rows, rows)
    high = own.astype(jnp.bfloat16)
    own = np.stack([high, (own - high.astype(np.float32)).astype(jnp.bfloat16)], axis=1)
    high = there.astype(jnp.bfloat16)
    low = there - high.astype(np.float32)
    coarse = np.concatenate([LOW_LIFT * low, there], axis=-1) * scale[:, None, None]
    coarse = coarse.astype(jnp.float8_e4m3fn)
    shape = (parts, parts - 1, 2 * rows)
    undo = [float(1.0 / (x * LOW_LIFT * COARSE_LIFT)) for x in scale]
    return own, high.reshape(shape + (rows,)), coarse.reshape(shape + (2 * rows,)), undo


def wall(operators, fields, v):
    rows = v.shape[1]
    side = jnp.concatenate([fields[0], fields[1]], axis=1)
    high = side.astype(jnp.bfloat16)
    low = (side - high.astype(jnp.float32)).astype(jnp.bfloat16)
    dot = functools.partial(jnp.dot, preferred_element_type=jnp.float32)
    product = dot(operators[0], high) + (dot(operators[1], high) + dot(operators[0], low))
    first, second = product[:rows], product[rows:]
    added = second - jnp.concatenate([v[0], v[1]], axis=1) * first
    return added[:, : v.shape[2]], added[:, v.shape[2] :]


def wall_there(undo, high_operators, coarse_operators, fields, v):
    rows = v.shape[1]
    side = jnp.concatenate([fields[0], fields[1]], axis=1)
    high = side.astype(jnp.bfloat16)
    low = side - high.astype(jnp.float32)
    coarse = jnp.concatenate(
        [
            (COARSE_LIFT * side).astype(jnp.float8_e4m3fn),
            (LOW_LIFT * COARSE_LIFT * low).astype(jnp.float8_e4m3fn),
        ],
        axis=0,
    )
    dot = functools.partial(jnp.dot, preferred_element_type=jnp.float32)
    product = dot(high_operators[...], high)
    rest = dot(coarse_operators[...], coarse)
    first = product[:rows] + undo[0] * rest[:rows]
    second = product[rows:] + undo[1] * rest[rows:]
    added = second - jnp.concatenate([v[0], v[1]], axis=1) * first
    return added[:, : v.shape[2]], added[:, v.shape[2] :]


def along_x(parity):
    return jnp.where(parity == 0, X_FIRST, -X_FIRST).astype(jnp.float32)


def local_kernel(blocks, velocity, previous, *refs):
    outs, parted = refs[:3], refs[3 : 3 + len(PIECES)]
    own, past, operators, came, sent = refs[3 + len(PIECES) :]
    me = lax.axis_index("gy")
    fetches = [
        pltpu.make_async_copy(velocity, own, came.at[0]),
        pltpu.make_async_copy(blocks.at[me], operators, came.at[1]),
        pltpu.make_async_copy(previous, past, came.at[2]),
    ]
    for fetch in fetches:
        fetch.start()
    fetches[0].wait()
    stores = [
        pltpu.make_async_copy(own.at[c[0] : c[-1] + 1], part, sent.at[i])
        for i, (c, part) in enumerate(zip(PIECES, parted))
    ]
    for store in stores:
        store.start()
    for fetch in fetches[1:]:
        fetch.wait()
    width = own.shape[3]
    roll = lambda f, k: pltpu.roll(f, k % width, 1)
    for q in range(3):
        added = wall(operators, own[q], own[1])
        for plane in range(2):
            f, other = own[q, plane], own[q, 1 - plane]
            u, w = own[0, plane], own[2, plane]
            step = X_FIRST if plane == 0 else -X_FIRST
            total = X_SECOND * (16.0 * other - 30.0 * f) - u * ((8.0 * step) * other)
            p1, m1, p2, m2 = roll(f, -1), roll(f, 1), roll(f, -2), roll(f, 2)
            total += Z_SECOND * (16.0 * (p1 + m1) - (p2 + m2) - 30.0 * f)
            total -= w * (Z_FIRST * (8.0 * (p1 - m1) - (p2 - m2)))
            outs[q][plane] = f + PAST * past[q, plane] + (total + added[plane])
    for store in stores:
        store.wait()


def near_kernel(velocity, *refs):
    near, refs = refs[: len(PIECES)], refs[len(PIECES) :]
    bases, outs, (u, slab, came) = refs[:3], refs[3:6], refs[6:]
    parity = lax.axis_index("gx") % 2
    inner, outer = 1 - parity, parity
    along = along_x(parity)
    fetches = [
        pltpu.make_async_copy(part.at[i], slab.at[q], came.at[q])
        for c, part in zip(PIECES, near)
        for i, q in enumerate(c)
    ]
    fetches.append(pltpu.make_async_copy(velocity.at[0], u, came.at[3]))
    for fetch in fetches:
        fetch.start()
    fetches[3].wait()
    for q in range(3):
        fetches[q].wait()
        base, out = bases[q], outs[q]
        first, second = slab[q, parity], slab[q, 1 - parity]
        out[outer] = base[outer] - X_SECOND * first + (along * u[outer]) * first
        out[inner] = (
            base[inner]
            + X_SECOND * (16.0 * first - second)
            - (along * u[inner]) * (8.0 * first - second)
        )


def far_terms(u):
    parity = lax.axis_index("gx") % 2
    inner, outer = 1 - parity, parity
    along = along_x(parity)
    inner_first = along * u[inner] + X_SECOND
    outer_second = along * u[outer] + X_SECOND
    outer_first = 8.0 * (outer_second + X_SECOND)

    def terms(far):
        first, second = far[1 - parity], far[parity]
        return (inner, -(inner_first * first)), (outer, outer_first * first - outer_second * second)

    return terms


def add(base, out, *terms):
    for plane, term in terms:
        out[plane] = base[plane] + term


def far_first(place):
    return (place + 1) // 2 % 2 == 1


def remote_kernel(undo, high_operators, coarse_operators, velocity, others, *refs):
    for q in range(3):
        terms = wall_there(undo, high_operators, coarse_operators, others[q], velocity[1])
        add(refs[q], refs[3 + q], *enumerate(terms))


def middle_kernel(undo, high_operators, coarse_operators, velocity, piece, *refs):
    bases, outs = refs[: len(refs) // 2], refs[len(refs) // 2 :]
    swapped = far_first(lax.axis_index("gx"))

    @pl.when(swapped)
    def _():
        for i, (base, out) in enumerate(zip(bases, outs)):
            terms = wall_there(undo, high_operators, coarse_operators, piece[i], velocity[1])
            add(base, out, *enumerate(terms))

    @pl.when(jnp.logical_not(swapped))
    def _():
        terms = far_terms(velocity.at[0])
        for i, (base, out) in enumerate(zip(bases, outs)):
            add(base, out, *terms(piece.at[i]))


def last_kernel(undo, high_operators, coarse_operators, velocity, whole, piece, *refs):
    bases, (out, total, sent) = refs[:3], refs[3:]
    swapped = far_first(lax.axis_index("gx"))
    rest = PIECES[-1]
    stores = [pltpu.make_async_copy(total.at[q], out.at[q], sent.at[q]) for q in range(3)]

    @pl.when(swapped)
    def _():
        terms = far_terms(velocity.at[0])
        for q in range(3):
            out = total.at[q]
            add(bases[q], out, *terms(whole.at[q]))
            if q in rest:
                field = piece[rest.index(q)]
                more = wall_there(undo, high_operators, coarse_operators, field, velocity[1])
                add(out, out, *enumerate(more))
            stores[q].start()

    @pl.when(jnp.logical_not(swapped))
    def _():
        terms = far_terms(velocity.at[0])
        for q in range(3):
            out = total.at[q]
            more = wall_there(undo, high_operators, coarse_operators, whole[q], velocity[1])
            add(bases[q], out, *enumerate(more))
            if q in rest:
                add(out, out, *terms(piece.at[rest.index(q)]))
            stores[q].start()

    for store in stores:
        store.wait()


VMEM = pl.BlockSpec(memory_space=pltpu.VMEM)
ANY = pl.BlockSpec(memory_space=pl.ANY)


def vmem(array):
    return pltpu.with_memory_space_constraint(array, pltpu.VMEM)


def hbm(array):
    return pltpu.with_memory_space_constraint(array, pltpu.HBM)


def call(kernel, ins, in_specs, out_shape, name, **kwargs):
    kwargs.setdefault("out_specs", jax.tree.map(lambda _: VMEM, out_shape))
    return pl.pallas_call(
        kernel,
        in_specs=in_specs,
        out_shape=out_shape,
        compiler_params=pltpu.CompilerParams(vmem_limit_bytes=VMEM_LIMIT),
        cost_estimate=pl.CostEstimate(flops=0, bytes_accessed=0, transcendentals=0),
        name=name,
        **kwargs,
    )(*ins)


def shards(parts, velocity, previous):
    count = lax.axis_size("gx")
    shape = velocity.shape
    assert shape[0] == 3 and shape[1] == 2 and count % 4 == 0
    rows = shape[2]
    me = lax.axis_index("gy")

    inward = [(i, i ^ 1) for i in range(count)]
    firsts, seconds = [], []
    for g in range(count):
        beyond = (g - 1) % count if g % 2 == 0 else (g + 1) % count
        for i in range(parts):
            here = g * parts + i
            pair = [(here, beyond * parts + i), (here, g * parts + (i + 1) % parts)]
            firsts.append(pair[0] if far_first(g) else pair[1])
            seconds.append(pair[1] if far_first(g) else pair[0])
    both = ("gx", "gy")
    first = lax.ppermute(velocity, both, firsts)
    others = [
        lax.ppermute(velocity, "gy", [(i, (i + k) % parts) for i in range(parts)])
        for k in range(2, parts)
    ]

    own, high, coarse, undo = operator_blocks(rows * parts, parts)
    own = jnp.asarray(own)
    high = lax.dynamic_index_in_dim(jnp.asarray(high), me, 0, keepdims=False)
    coarse = lax.dynamic_index_in_dim(jnp.asarray(coarse), me, 0, keepdims=False)

    one = jax.ShapeDtypeStruct(shape[1:], jnp.float32)
    whole = jax.ShapeDtypeStruct(shape, jnp.float32)
    totals = call(
        local_kernel,
        (hbm(own), hbm(velocity), hbm(previous)),
        [ANY] * 3,
        (one,) * 3
        + tuple(jax.ShapeDtypeStruct((len(c),) + shape[1:], jnp.float32) for c in PIECES),
        "local",
        out_specs=(VMEM,) * 3 + (ANY,) * len(PIECES),
        scratch_shapes=[
            pltpu.VMEM(shape, jnp.float32),
            pltpu.VMEM(shape, jnp.float32),
            pltpu.VMEM(own.shape[1:], jnp.bfloat16),
            pltpu.SemaphoreType.DMA((3,)),
            pltpu.SemaphoreType.DMA((len(PIECES),)),
        ],
    )
    near = [lax.ppermute(part, "gx", inward) for part in totals[3:]]
    second = [lax.ppermute(part, both, seconds) for part in totals[3:]]
    totals = call(
        near_kernel,
        (hbm(velocity), *map(hbm, near), *totals[:3]),
        [ANY] * (1 + len(PIECES)) + [VMEM] * 3,
        (one,) * 3,
        "near",
        scratch_shapes=[
            pltpu.VMEM(shape[1:], jnp.float32),
            pltpu.VMEM(shape, jnp.float32),
            pltpu.SemaphoreType.DMA((4,)),
        ],
    )
    for k in range(2, parts):
        totals = call(
            functools.partial(remote_kernel, undo),
            (high[k - 1], coarse[k - 1], velocity, others[k - 2], *totals),
            [VMEM] * 7,
            (one,) * 3,
            "remote",
        )
    totals = list(totals)
    fixed = (vmem(high[0]), vmem(coarse[0]), vmem(velocity))
    for c, piece in zip(PIECES[:-1], second):
        added = call(
            functools.partial(middle_kernel, undo),
            (*fixed, piece, *(totals[q] for q in c)),
            [VMEM] * (4 + len(c)),
            (one,) * len(c),
            "middle",
        )
        for q, total in zip(c, added):
            totals[q] = total
    return call(
        functools.partial(last_kernel, undo),
        (*fixed, vmem(first), vmem(second[-1]), *totals),
        [VMEM] * 8,
        whole,
        "last",
        out_specs=ANY,
        scratch_shapes=[pltpu.VMEM(shape, jnp.float32), pltpu.SemaphoreType.DMA((3,))],
    )


def solution(mesh):
    spec = P(None, "gx", "gy", None)
    body = functools.partial(shards, mesh.shape["gy"])
    return jax.shard_map(body, mesh=mesh, in_specs=(spec, spec), out_specs=spec, check_vma=False)
```

```python
import functools

import jax
import jax.numpy as jnp
import numpy as np
from jax import lax
from jax.experimental import pallas as pl
from jax.experimental.pallas import tpu as pltpu
from jax.sharding import PartitionSpec as P

NY = 1024


LENGTH_SPACING = 8.0 * 3.141592653589793 / 4096.0
SPAN_SPACING = 3.0 * 3.141592653589793 / 3072.0
VISCOSITY = 1.0 / 2000.0
TIME_STEP = 0.003
GAMMA_NOW = 5.0 / 12.0
ZETA_PAST = -17.0 / 60.0

SCALE = TIME_STEP * GAMMA_NOW
X_FIRST = SCALE / (12.0 * LENGTH_SPACING)
X_SECOND = SCALE * VISCOSITY / (12.0 * LENGTH_SPACING * LENGTH_SPACING)
Z_FIRST = SCALE / (12.0 * SPAN_SPACING)
Z_SECOND = SCALE * VISCOSITY / (12.0 * SPAN_SPACING * SPAN_SPACING)
PAST = TIME_STEP * ZETA_PAST

VMEM_LIMIT = 24 * 1024 * 1024
PIECES = ((0, 1), (2,))
COARSE_LARGEST = 224.0
COARSE_LIFT = 32.0
LOW_LIFT = 512.0


def chebyshev_matrices(total):
    one = np.float32(1.0)
    ids = np.arange(total, dtype=np.int32)
    angle = ids.astype(np.float32) * (np.float32(np.pi) / np.float32(total - 1))
    on_diagonal = ids[:, None] == ids[None, :]
    signs = one - np.float32(2.0) * ((ids[:, None] + ids[None, :]) % 2).astype(np.float32)
    half = np.where((ids == 0) | (ids == total - 1), 0.5, 1.0).astype(np.float32)
    weight_ratio = signs * half[None, :] / half[:, None]
    spacing = (
        np.float32(-2.0)
        * np.sin(np.float32(0.5) * (angle[:, None] + angle[None, :]))
        * np.sin(np.float32(0.5) * (angle[:, None] - angle[None, :]))
    )
    spacing = np.where(on_diagonal, one, spacing)
    first = np.where(on_diagonal, np.float32(0.0), weight_ratio / spacing)
    first_diag = -np.sum(first, axis=1, dtype=np.float32)
    second = np.where(
        on_diagonal,
        np.float32(0.0),
        np.float32(2.0) * first * (first_diag[:, None] - one / spacing),
    )
    second_diag = -np.sum(second, axis=1, dtype=np.float32)
    first[ids, ids] = first_diag
    second[ids, ids] = second_diag
    return first, second


def operator_blocks(total, parts):
    first, second = chebyshev_matrices(total)
    rows = total // parts
    stacked = np.stack(
        [first.astype(np.float64) * SCALE, second.astype(np.float64) * (SCALE * VISCOSITY)]
    ).astype(np.float32)
    blocks = stacked.reshape(2, parts, rows, parts, rows).transpose(1, 3, 0, 2, 4)
    mine = np.arange(parts)
    own = blocks[mine, mine]
    there = np.stack([blocks[mine, (mine - k) % parts] for k in range(1, parts)], axis=1)
    largest = np.max(np.abs(there), axis=(0, 1, 3, 4))
    scale = np.exp2(np.floor(np.log2(COARSE_LARGEST / largest))).astype(np.float32)
    own = own.reshape(parts, 2 * rows, rows)
    high = own.astype(jnp.bfloat16)
    own = np.stack([high, (own - high.astype(np.float32)).astype(jnp.bfloat16)], axis=1)
    high = there.astype(jnp.bfloat16)
    low = there - high.astype(np.float32)
    coarse = np.concatenate([LOW_LIFT * low, there], axis=-1) * scale[:, None, None]
    coarse = coarse.astype(jnp.float8_e4m3fn)
    shape = (parts, parts - 1, 2 * rows)
    undo = [float(1.0 / (x * LOW_LIFT * COARSE_LIFT)) for x in scale]
    return own, high.reshape(shape + (rows,)), coarse.reshape(shape + (2 * rows,)), undo


def wall(operators, fields, v):
    rows = v.shape[1]
    side = jnp.concatenate([fields[0], fields[1]], axis=1)
    high = side.astype(jnp.bfloat16)
    low = (side - high.astype(jnp.float32)).astype(jnp.bfloat16)
    dot = functools.partial(jnp.dot, preferred_element_type=jnp.float32)
    product = dot(operators[0], high) + (dot(operators[1], high) + dot(operators[0], low))
    first, second = product[:rows], product[rows:]
    added = second - jnp.concatenate([v[0], v[1]], axis=1) * first
    return added[:, : v.shape[2]], added[:, v.shape[2] :]


def parted_field(fields):
    side = jnp.concatenate([fields[0], fields[1]], axis=1)
    high = side.astype(jnp.bfloat16)
    low = side - high.astype(jnp.float32)
    coarse = jnp.concatenate(
        [
            (COARSE_LIFT * side).astype(jnp.float8_e4m3fn),
            (LOW_LIFT * COARSE_LIFT * low).astype(jnp.float8_e4m3fn),
        ],
        axis=0,
    )
    return high, coarse


def wall_rows(undo, operators, field, v, start, count):
    rows = v.shape[1]
    dot = functools.partial(jnp.dot, preferred_element_type=jnp.float32)
    sums = []
    for matrix in range(2):
        at = pl.ds(matrix * rows + start, count)
        products = [dot(operator[at], part) for operator, part in zip(operators, field)]
        sums.append(products[0] + undo[matrix] * products[1])
    at = pl.ds(start, count)
    added = sums[1] - jnp.concatenate([v[0, at], v[1, at]], axis=1) * sums[0]
    return added[:, : v.shape[2]], added[:, v.shape[2] :]


def wall_there(undo, high_operators, coarse_operators, fields, v):
    operators = (high_operators, coarse_operators)
    return wall_rows(undo, operators, parted_field(fields), v, 0, v.shape[1])


def along_x(parity):
    return jnp.where(parity == 0, X_FIRST, -X_FIRST).astype(jnp.float32)


def local_kernel(blocks, velocity, previous, *refs):
    outs, parted = refs[:3], refs[3 : 3 + len(PIECES)]
    own, past, operators, came, sent = refs[3 + len(PIECES) :]
    me = lax.axis_index("gy")
    fetches = [
        pltpu.make_async_copy(velocity, own, came.at[0]),
        pltpu.make_async_copy(blocks.at[me], operators, came.at[1]),
        pltpu.make_async_copy(previous, past, came.at[2]),
    ]
    for fetch in fetches:
        fetch.start()
    fetches[0].wait()
    stores = [
        pltpu.make_async_copy(own.at[c[0] : c[-1] + 1], part, sent.at[i])
        for i, (c, part) in enumerate(zip(PIECES, parted))
    ]
    for store in stores:
        store.start()
    for fetch in fetches[1:]:
        fetch.wait()
    width = own.shape[3]
    roll = lambda f, k: pltpu.roll(f, k % width, 1)
    for q in range(3):
        added = wall(operators, own[q], own[1])
        for plane in range(2):
            f, other = own[q, plane], own[q, 1 - plane]
            u, w = own[0, plane], own[2, plane]
            step = X_FIRST if plane == 0 else -X_FIRST
            total = X_SECOND * (16.0 * other - 30.0 * f) - u * ((8.0 * step) * other)
            p1, m1, p2, m2 = roll(f, -1), roll(f, 1), roll(f, -2), roll(f, 2)
            total += Z_SECOND * (16.0 * (p1 + m1) - (p2 + m2) - 30.0 * f)
            total -= w * (Z_FIRST * (8.0 * (p1 - m1) - (p2 - m2)))
            outs[q][plane] = f + PAST * past[q, plane] + (total + added[plane])
    for store in stores:
        store.wait()


def near_kernel(velocity, *refs):
    near, refs = refs[: len(PIECES)], refs[len(PIECES) :]
    bases, outs, (u, slab, came) = refs[:3], refs[3:6], refs[6:]
    parity = lax.axis_index("gx") % 2
    inner, outer = 1 - parity, parity
    along = along_x(parity)
    fetches = [
        pltpu.make_async_copy(part.at[i], slab.at[q], came.at[q])
        for c, part in zip(PIECES, near)
        for i, q in enumerate(c)
    ]
    fetches.append(pltpu.make_async_copy(velocity.at[0], u, came.at[3]))
    for fetch in fetches:
        fetch.start()
    fetches[3].wait()
    for q in range(3):
        fetches[q].wait()
        base, out = bases[q], outs[q]
        first, second = slab[q, parity], slab[q, 1 - parity]
        out[outer] = base[outer] - X_SECOND * first + (along * u[outer]) * first
        out[inner] = (
            base[inner]
            + X_SECOND * (16.0 * first - second)
            - (along * u[inner]) * (8.0 * first - second)
        )


def far_terms(u):
    parity = lax.axis_index("gx") % 2
    inner, outer = 1 - parity, parity
    along = along_x(parity)
    inner_first = along * u[inner] + X_SECOND
    outer_second = along * u[outer] + X_SECOND
    outer_first = 8.0 * (outer_second + X_SECOND)

    def terms(far):
        first, second = far[1 - parity], far[parity]
        return (inner, -(inner_first * first)), (outer, outer_first * first - outer_second * second)

    return terms


def add(base, out, *terms):
    for plane, term in terms:
        out[plane] = base[plane] + term


def far_first(place):
    return (place + 1) // 2 % 2 == 1


def remote_kernel(undo, high_operators, coarse_operators, velocity, others, *refs):
    for q in range(3):
        terms = wall_there(undo, high_operators, coarse_operators, others[q], velocity.at[1])
        add(refs[q], refs[3 + q], *enumerate(terms))


def middle_kernel(undo, high_operators, coarse_operators, velocity, piece, *refs):
    bases, outs = refs[: len(refs) // 2], refs[len(refs) // 2 :]
    swapped = far_first(lax.axis_index("gx"))

    @pl.when(swapped)
    def _():
        for i, (base, out) in enumerate(zip(bases, outs)):
            terms = wall_there(undo, high_operators, coarse_operators, piece[i], velocity.at[1])
            add(base, out, *enumerate(terms))

    @pl.when(jnp.logical_not(swapped))
    def _():
        terms = far_terms(velocity.at[0])
        for i, (base, out) in enumerate(zip(bases, outs)):
            add(base, out, *terms(piece.at[i]))


def first_kernel(undo, high_operators, coarse_operators, velocity, whole, *refs):
    bases, outs = refs[:3], refs[3:]
    swapped = far_first(lax.axis_index("gx"))

    @pl.when(swapped)
    def _():
        terms = far_terms(velocity.at[0])
        for q in range(3):
            add(bases[q], outs[q], *terms(whole.at[q]))

    @pl.when(jnp.logical_not(swapped))
    def _():
        for q in range(3):
            terms = wall_there(undo, high_operators, coarse_operators, whole[q], velocity.at[1])
            add(bases[q], outs[q], *enumerate(terms))


def last_kernel(undo, high_operators, coarse_operators, velocity, piece, *refs):
    bases, (out, total, sent) = refs[:3], refs[3:]
    swapped = far_first(lax.axis_index("gx"))
    (last,) = PIECES[-1]
    operators = (high_operators, coarse_operators)
    half = velocity.shape[2] // 2
    ready = [q for q in range(3) if q != last]
    stores = [pltpu.make_async_copy(bases[q], out.at[q], sent.at[q]) for q in ready]
    for store in stores:
        store.start()
    for i in range(2):
        at = pl.ds(i * half, half)
        stores.append(pltpu.make_async_copy(total.at[:, at], out.at[last, :, at], sent.at[3 + i]))

    @pl.when(swapped)
    def _():
        field = parted_field(piece[0])
        for i in range(2):
            at = pl.ds(i * half, half)
            more = wall_rows(undo, operators, field, velocity.at[1], i * half, half)
            for plane in range(2):
                total[plane, at] = bases[last][plane, at] + more[plane]
            stores[2 + i].start()

    @pl.when(jnp.logical_not(swapped))
    def _():
        add(bases[last], total, *far_terms(velocity.at[0])(piece.at[0]))
        for i in range(2):
            stores[2 + i].start()

    for store in stores:
        store.wait()


VMEM = pl.BlockSpec(memory_space=pltpu.VMEM)
ANY = pl.BlockSpec(memory_space=pl.ANY)


def vmem(array):
    return pltpu.with_memory_space_constraint(array, pltpu.VMEM)


def hbm(array):
    return pltpu.with_memory_space_constraint(array, pltpu.HBM)


def call(kernel, ins, in_specs, out_shape, name, **kwargs):
    kwargs.setdefault("out_specs", jax.tree.map(lambda _: VMEM, out_shape))
    return pl.pallas_call(
        kernel,
        in_specs=in_specs,
        out_shape=out_shape,
        compiler_params=pltpu.CompilerParams(vmem_limit_bytes=VMEM_LIMIT),
        cost_estimate=pl.CostEstimate(flops=0, bytes_accessed=0, transcendentals=0),
        name=name,
        **kwargs,
    )(*ins)


def shards(parts, velocity, previous):
    count = lax.axis_size("gx")
    shape = velocity.shape
    assert shape[0] == 3 and shape[1] == 2 and count % 4 == 0
    rows = shape[2]
    me = lax.axis_index("gy")

    inward = [(i, i ^ 1) for i in range(count)]
    firsts, seconds = [], []
    for g in range(count):
        beyond = (g - 1) % count if g % 2 == 0 else (g + 1) % count
        for i in range(parts):
            here = g * parts + i
            pair = [(here, beyond * parts + i), (here, g * parts + (i + 1) % parts)]
            firsts.append(pair[0] if far_first(g) else pair[1])
            seconds.append(pair[1] if far_first(g) else pair[0])
    both = ("gx", "gy")
    first = lax.ppermute(velocity, both, firsts)
    others = [
        lax.ppermute(velocity, "gy", [(i, (i + k) % parts) for i in range(parts)])
        for k in range(2, parts)
    ]

    own, high, coarse, undo = operator_blocks(rows * parts, parts)
    own = jnp.asarray(own)
    high = lax.dynamic_index_in_dim(jnp.asarray(high), me, 0, keepdims=False)
    coarse = lax.dynamic_index_in_dim(jnp.asarray(coarse), me, 0, keepdims=False)

    one = jax.ShapeDtypeStruct(shape[1:], jnp.float32)
    whole = jax.ShapeDtypeStruct(shape, jnp.float32)
    totals = call(
        local_kernel,
        (hbm(own), hbm(velocity), hbm(previous)),
        [ANY] * 3,
        (one,) * 3
        + tuple(jax.ShapeDtypeStruct((len(c),) + shape[1:], jnp.float32) for c in PIECES),
        "local",
        out_specs=(VMEM,) * 3 + (ANY,) * len(PIECES),
        scratch_shapes=[
            pltpu.VMEM(shape, jnp.float32),
            pltpu.VMEM(shape, jnp.float32),
            pltpu.VMEM(own.shape[1:], jnp.bfloat16),
            pltpu.SemaphoreType.DMA((3,)),
            pltpu.SemaphoreType.DMA((len(PIECES),)),
        ],
    )
    near = [lax.ppermute(part, "gx", inward) for part in totals[3:]]
    second = [lax.ppermute(part, both, seconds) for part in totals[3:]]
    totals = call(
        near_kernel,
        (hbm(velocity), *map(hbm, near), *totals[:3]),
        [ANY] * (1 + len(PIECES)) + [VMEM] * 3,
        (one,) * 3,
        "near",
        scratch_shapes=[
            pltpu.VMEM(shape[1:], jnp.float32),
            pltpu.VMEM(shape, jnp.float32),
            pltpu.SemaphoreType.DMA((4,)),
        ],
    )
    for k in range(2, parts):
        totals = call(
            functools.partial(remote_kernel, undo),
            (high[k - 1], coarse[k - 1], velocity, others[k - 2], *totals),
            [VMEM] * 7,
            (one,) * 3,
            "remote",
        )
    totals = list(totals)
    fixed = (vmem(high[0]), vmem(coarse[0]), vmem(velocity))
    for c, piece in zip(PIECES[:-1], second):
        added = call(
            functools.partial(middle_kernel, undo),
            (*fixed, piece, *(totals[q] for q in c)),
            [VMEM] * (4 + len(c)),
            (one,) * len(c),
            "middle",
        )
        for q, total in zip(c, added):
            totals[q] = total
    totals = call(
        functools.partial(first_kernel, undo),
        (*fixed, vmem(first), *totals),
        [VMEM] * 7,
        (one,) * 3,
        "first",
    )
    return call(
        functools.partial(last_kernel, undo),
        (*fixed, vmem(second[-1]), *totals),
        [VMEM] * 7,
        whole,
        "last",
        out_specs=ANY,
        scratch_shapes=[pltpu.VMEM(shape[1:], jnp.float32), pltpu.SemaphoreType.DMA((5,))],
    )


def solution(mesh):
    spec = P(None, "gx", "gy", None)
    body = functools.partial(shards, mesh.shape["gy"])
    return jax.shard_map(body, mesh=mesh, in_specs=(spec, spec), out_specs=spec, check_vma=False)
```

```python
import functools

import jax
import jax.numpy as jnp
import numpy as np
from jax import lax
from jax.experimental import pallas as pl
from jax.experimental.pallas import tpu as pltpu
from jax.sharding import PartitionSpec as P

NY = 1024


LENGTH_SPACING = 8.0 * 3.141592653589793 / 4096.0
SPAN_SPACING = 3.0 * 3.141592653589793 / 3072.0
VISCOSITY = 1.0 / 2000.0
TIME_STEP = 0.003
GAMMA_NOW = 5.0 / 12.0
ZETA_PAST = -17.0 / 60.0

SCALE = TIME_STEP * GAMMA_NOW
X_FIRST = SCALE / (12.0 * LENGTH_SPACING)
X_SECOND = SCALE * VISCOSITY / (12.0 * LENGTH_SPACING * LENGTH_SPACING)
Z_FIRST = SCALE / (12.0 * SPAN_SPACING)
Z_SECOND = SCALE * VISCOSITY / (12.0 * SPAN_SPACING * SPAN_SPACING)
PAST = TIME_STEP * ZETA_PAST

VMEM_LIMIT = 24 * 1024 * 1024
PIECES = ((0, 1), (2,))
LAST = 2
COARSE_LARGEST = 224.0
COARSE_LIFT = 32.0
LOW_LIFT = 512.0


def chebyshev_matrices(total):
    one = np.float32(1.0)
    ids = np.arange(total, dtype=np.int32)
    angle = ids.astype(np.float32) * (np.float32(np.pi) / np.float32(total - 1))
    on_diagonal = ids[:, None] == ids[None, :]
    signs = one - np.float32(2.0) * ((ids[:, None] + ids[None, :]) % 2).astype(np.float32)
    half = np.where((ids == 0) | (ids == total - 1), 0.5, 1.0).astype(np.float32)
    weight_ratio = signs * half[None, :] / half[:, None]
    spacing = (
        np.float32(-2.0)
        * np.sin(np.float32(0.5) * (angle[:, None] + angle[None, :]))
        * np.sin(np.float32(0.5) * (angle[:, None] - angle[None, :]))
    )
    spacing = np.where(on_diagonal, one, spacing)
    first = np.where(on_diagonal, np.float32(0.0), weight_ratio / spacing)
    first_diag = -np.sum(first, axis=1, dtype=np.float32)
    second = np.where(
        on_diagonal,
        np.float32(0.0),
        np.float32(2.0) * first * (first_diag[:, None] - one / spacing),
    )
    second_diag = -np.sum(second, axis=1, dtype=np.float32)
    first[ids, ids] = first_diag
    second[ids, ids] = second_diag
    return first, second


def operator_blocks(total, parts):
    first, second = chebyshev_matrices(total)
    rows = total // parts
    stacked = np.stack(
        [first.astype(np.float64) * SCALE, second.astype(np.float64) * (SCALE * VISCOSITY)]
    ).astype(np.float32)
    blocks = stacked.reshape(2, parts, rows, parts, rows).transpose(1, 3, 0, 2, 4)
    mine = np.arange(parts)
    own = blocks[mine, mine]
    there = np.stack([blocks[mine, (mine - k) % parts] for k in range(1, parts)], axis=1)
    largest = np.max(np.abs(there), axis=(0, 1, 3, 4))
    scale = np.exp2(np.floor(np.log2(COARSE_LARGEST / largest))).astype(np.float32)
    own = own.reshape(parts, 2 * rows, rows)
    high = own.astype(jnp.bfloat16)
    own = np.stack([high, (own - high.astype(np.float32)).astype(jnp.bfloat16)], axis=1)
    high = there.astype(jnp.bfloat16)
    low = there - high.astype(np.float32)
    coarse = np.concatenate([LOW_LIFT * low, there], axis=-1) * scale[:, None, None]
    coarse = coarse.astype(jnp.float8_e4m3fn)
    shape = (parts, parts - 1, 2 * rows)
    undo = [float(1.0 / (x * LOW_LIFT * COARSE_LIFT)) for x in scale]
    return own, high.reshape(shape + (rows,)), coarse.reshape(shape + (2 * rows,)), undo


def wall(operators, fields, v):
    rows = v.shape[1]
    side = jnp.concatenate([fields[0], fields[1]], axis=1)
    high = side.astype(jnp.bfloat16)
    low = (side - high.astype(jnp.float32)).astype(jnp.bfloat16)
    dot = functools.partial(jnp.dot, preferred_element_type=jnp.float32)
    product = dot(operators[0], high) + (dot(operators[1], high) + dot(operators[0], low))
    first, second = product[:rows], product[rows:]
    added = second - jnp.concatenate([v[0], v[1]], axis=1) * first
    return added[:, : v.shape[2]], added[:, v.shape[2] :]


def second_pieces(rows):
    early = rows * 3 // 4 if rows % 512 == 0 else rows
    pieces = [((0, 1), 0, rows), ((LAST,), 0, early), ((LAST,), early, rows - early)]
    return [piece for piece in pieces if piece[2]]


def parted_field(fields):
    side = jnp.concatenate([fields[0], fields[1]], axis=1)
    high = side.astype(jnp.bfloat16)
    low = side - high.astype(jnp.float32)
    values = (COARSE_LIFT * side).astype(jnp.float8_e4m3fn)
    return high, values, (LOW_LIFT * COARSE_LIFT * low).astype(jnp.float8_e4m3fn)


def wall_rows(undo, operators, field, v, start, count, begin=0):
    rows = v.shape[1]
    (high_operators, coarse_operators), (high, values, lows) = operators, field
    depth = high.shape[0]
    dot = functools.partial(jnp.dot, preferred_element_type=jnp.float32)
    sums = []
    for matrix in range(2):
        at = pl.ds(matrix * rows + start, count)
        product = dot(high_operators[at, begin : begin + depth], high)
        if depth == rows:
            rest = dot(coarse_operators[at], jnp.concatenate([values, lows], axis=0))
        else:
            rest = dot(coarse_operators[at, begin : begin + depth], values)
            rest += dot(coarse_operators[at, rows + begin : rows + begin + depth], lows)
        sums.append(product + undo[matrix] * rest)
    at = pl.ds(start, count)
    added = sums[1] - jnp.concatenate([v[0, at], v[1, at]], axis=1) * sums[0]
    return added[:, : v.shape[2]], added[:, v.shape[2] :]


def wall_there(undo, high_operators, coarse_operators, fields, v, begin=0):
    operators = (high_operators, coarse_operators)
    return wall_rows(undo, operators, parted_field(fields), v, 0, v.shape[1], begin)


def along_x(parity):
    return jnp.where(parity == 0, X_FIRST, -X_FIRST).astype(jnp.float32)


def local_kernel(cuts, blocks, velocity, previous, *refs):
    outs, parted, (own, past, operators, came, sent) = refs[:3], refs[3:-5], refs[-5:]
    me = lax.axis_index("gy")
    fetches = [
        pltpu.make_async_copy(velocity, own, came.at[0]),
        pltpu.make_async_copy(blocks.at[me], operators, came.at[1]),
        pltpu.make_async_copy(previous, past, came.at[2]),
    ]
    for fetch in fetches:
        fetch.start()
    fetches[0].wait()
    stores = [
        pltpu.make_async_copy(own.at[c[0] : c[-1] + 1, :, pl.ds(begin, count)], part, sent.at[i])
        for i, ((c, begin, count), part) in enumerate(zip(cuts, parted))
    ]
    for store in stores:
        store.start()
    for fetch in fetches[1:]:
        fetch.wait()
    width = own.shape[3]
    roll = lambda f, k: pltpu.roll(f, k % width, 1)
    for q in range(3):
        added = wall(operators, own[q], own[1])
        for plane in range(2):
            f, other = own[q, plane], own[q, 1 - plane]
            u, w = own[0, plane], own[2, plane]
            step = X_FIRST if plane == 0 else -X_FIRST
            total = X_SECOND * (16.0 * other - 30.0 * f) - u * ((8.0 * step) * other)
            p1, m1, p2, m2 = roll(f, -1), roll(f, 1), roll(f, -2), roll(f, 2)
            total += Z_SECOND * (16.0 * (p1 + m1) - (p2 + m2) - 30.0 * f)
            total -= w * (Z_FIRST * (8.0 * (p1 - m1) - (p2 - m2)))
            outs[q][plane] = f + PAST * past[q, plane] + (total + added[plane])
    for store in stores:
        store.wait()


def near_kernel(velocity, *refs):
    near, refs = refs[: len(PIECES)], refs[len(PIECES) :]
    bases, outs, (u, slab, came) = refs[:3], refs[3:6], refs[6:]
    parity = lax.axis_index("gx") % 2
    inner, outer = 1 - parity, parity
    along = along_x(parity)
    fetches = [
        pltpu.make_async_copy(part.at[i], slab.at[q], came.at[q])
        for c, part in zip(PIECES, near)
        for i, q in enumerate(c)
    ]
    fetches.append(pltpu.make_async_copy(velocity.at[0], u, came.at[3]))
    for fetch in fetches:
        fetch.start()
    fetches[3].wait()
    for q in range(3):
        fetches[q].wait()
        base, out = bases[q], outs[q]
        first, second = slab[q, parity], slab[q, 1 - parity]
        out[outer] = base[outer] - X_SECOND * first + (along * u[outer]) * first
        out[inner] = (
            base[inner]
            + X_SECOND * (16.0 * first - second)
            - (along * u[inner]) * (8.0 * first - second)
        )


def far_terms(u):
    parity = lax.axis_index("gx") % 2
    inner, outer = 1 - parity, parity
    along = along_x(parity)
    inner_first = along * u[inner] + X_SECOND
    outer_second = along * u[outer] + X_SECOND
    outer_first = 8.0 * (outer_second + X_SECOND)

    def terms(far):
        first, second = far[1 - parity], far[parity]
        return (inner, -(inner_first * first)), (outer, outer_first * first - outer_second * second)

    return terms


def add(base, out, *terms):
    for plane, term in terms:
        out[plane] = base[plane] + term


def far_first(place):
    return (place + 1) // 2 % 2 == 1


def remote_kernel(undo, high_operators, coarse_operators, velocity, others, *refs):
    for q in range(3):
        terms = wall_there(undo, high_operators, coarse_operators, others[q], velocity.at[1])
        add(refs[q], refs[3 + q], *enumerate(terms))


def middle_kernel(undo, begin, count, high_operators, coarse_operators, velocity, piece, *refs):
    bases, outs = refs[:count], refs[-count:]
    swapped = far_first(lax.axis_index("gx"))
    at = pl.ds(begin, piece.shape[2])

    @pl.when(swapped)
    def _():
        for i, (base, out) in enumerate(zip(bases, outs)):
            terms = wall_there(
                undo, high_operators, coarse_operators, piece[i], velocity.at[1], begin
            )
            add(base, out, *enumerate(terms))

    @pl.when(jnp.logical_not(swapped))
    def _():
        terms = far_terms(velocity.at[0, :, at])
        for i, (base, out) in enumerate(zip(bases, outs)):
            if piece.shape[2] < out.shape[1]:
                out[...] = base[...]
            add(base.at[:, at], out.at[:, at], *terms(piece.at[i]))


def first_kernel(undo, high_operators, coarse_operators, velocity, whole, *refs):
    bases, outs = refs[:3], refs[3:]
    swapped = far_first(lax.axis_index("gx"))

    @pl.when(swapped)
    def _():
        terms = far_terms(velocity.at[0])
        for q in range(3):
            add(bases[q], outs[q], *terms(whole.at[q]))

    @pl.when(jnp.logical_not(swapped))
    def _():
        for q in range(3):
            terms = wall_there(undo, high_operators, coarse_operators, whole[q], velocity.at[1])
            add(bases[q], outs[q], *enumerate(terms))


def last_kernel(undo, begin, high_operators, coarse_operators, velocity, piece, *refs):
    bases, (out, total, sent) = refs[:3], refs[3:]
    swapped = far_first(lax.axis_index("gx"))
    operators = (high_operators, coarse_operators)
    half = velocity.shape[2] // 2
    ready = [q for q in range(3) if q != LAST]
    stores = [pltpu.make_async_copy(bases[q], out.at[q], sent.at[q]) for q in ready]
    for store in stores:
        store.start()
    for i in range(2):
        at = pl.ds(i * half, half)
        stores.append(pltpu.make_async_copy(total.at[:, at], out.at[LAST, :, at], sent.at[3 + i]))

    @pl.when(swapped)
    def _():
        field = parted_field(piece[0])
        for i in range(2):
            at = pl.ds(i * half, half)
            more = wall_rows(undo, operators, field, velocity.at[1], i * half, half, begin)
            for plane in range(2):
                total[plane, at] = bases[LAST][plane, at] + more[plane]
            stores[2 + i].start()

    @pl.when(jnp.logical_not(swapped))
    def _():
        at = pl.ds(begin, piece.shape[2])
        total[...] = bases[LAST][...]
        terms = far_terms(velocity.at[0, :, at])
        add(bases[LAST].at[:, at], total.at[:, at], *terms(piece.at[0]))
        for i in range(2):
            stores[2 + i].start()

    for store in stores:
        store.wait()


VMEM = pl.BlockSpec(memory_space=pltpu.VMEM)
ANY = pl.BlockSpec(memory_space=pl.ANY)


def vmem(array):
    return pltpu.with_memory_space_constraint(array, pltpu.VMEM)


def hbm(array):
    return pltpu.with_memory_space_constraint(array, pltpu.HBM)


def call(kernel, ins, in_specs, out_shape, name, **kwargs):
    kwargs.setdefault("out_specs", jax.tree.map(lambda _: VMEM, out_shape))
    return pl.pallas_call(
        kernel,
        in_specs=in_specs,
        out_shape=out_shape,
        compiler_params=pltpu.CompilerParams(vmem_limit_bytes=VMEM_LIMIT),
        cost_estimate=pl.CostEstimate(flops=0, bytes_accessed=0, transcendentals=0),
        name=name,
        **kwargs,
    )(*ins)


def shards(parts, velocity, previous):
    count = lax.axis_size("gx")
    shape = velocity.shape
    assert shape[0] == 3 and shape[1] == 2 and count % 4 == 0
    rows = shape[2]
    me = lax.axis_index("gy")

    inward = [(i, i ^ 1) for i in range(count)]
    firsts, seconds = [], []
    for g in range(count):
        beyond = (g - 1) % count if g % 2 == 0 else (g + 1) % count
        for i in range(parts):
            here = g * parts + i
            pair = [(here, beyond * parts + i), (here, g * parts + (i + 1) % parts)]
            firsts.append(pair[0] if far_first(g) else pair[1])
            seconds.append(pair[1] if far_first(g) else pair[0])
    both = ("gx", "gy")
    first = lax.ppermute(velocity, both, firsts)
    others = [
        lax.ppermute(velocity, "gy", [(i, (i + k) % parts) for i in range(parts)])
        for k in range(2, parts)
    ]

    own, high, coarse, undo = operator_blocks(rows * parts, parts)
    own = jnp.asarray(own)
    high = lax.dynamic_index_in_dim(jnp.asarray(high), me, 0, keepdims=False)
    coarse = lax.dynamic_index_in_dim(jnp.asarray(coarse), me, 0, keepdims=False)

    one = jax.ShapeDtypeStruct(shape[1:], jnp.float32)
    whole = jax.ShapeDtypeStruct(shape, jnp.float32)
    pieces = second_pieces(rows)
    cuts = [(c, 0, rows) for c in PIECES]
    cuts += [piece for piece in pieces if piece not in cuts]
    made = call(
        functools.partial(local_kernel, cuts),
        (hbm(own), hbm(velocity), hbm(previous)),
        [ANY] * 3,
        (one,) * 3
        + tuple(
            jax.ShapeDtypeStruct((len(c), shape[1], n, shape[3]), jnp.float32) for c, _, n in cuts
        ),
        "local",
        out_specs=(VMEM,) * 3 + (ANY,) * len(cuts),
        scratch_shapes=[
            pltpu.VMEM(shape, jnp.float32),
            pltpu.VMEM(shape, jnp.float32),
            pltpu.VMEM(own.shape[1:], jnp.bfloat16),
            pltpu.SemaphoreType.DMA((3,)),
            pltpu.SemaphoreType.DMA((len(cuts),)),
        ],
    )
    totals, parted = made[:3], made[3:]
    near = [lax.ppermute(part, "gx", inward) for part in parted[: len(PIECES)]]
    second = [lax.ppermute(parted[cuts.index(piece)], both, seconds) for piece in pieces]
    totals = call(
        near_kernel,
        (hbm(velocity), *map(hbm, near), *totals),
        [ANY] * (1 + len(PIECES)) + [VMEM] * 3,
        (one,) * 3,
        "near",
        scratch_shapes=[
            pltpu.VMEM(shape[1:], jnp.float32),
            pltpu.VMEM(shape, jnp.float32),
            pltpu.SemaphoreType.DMA((4,)),
        ],
    )
    for k in range(2, parts):
        totals = call(
            functools.partial(remote_kernel, undo),
            (high[k - 1], coarse[k - 1], velocity, others[k - 2], *totals),
            [VMEM] * 7,
            (one,) * 3,
            "remote",
        )
    totals = list(totals)
    fixed = (vmem(high[0]), vmem(coarse[0]), vmem(velocity))
    behind = ()
    for (c, begin, _), piece in zip(pieces[:-1], second):
        added = call(
            functools.partial(middle_kernel, undo, begin, len(c)),
            (*fixed, piece, *(totals[q] for q in c), *behind),
            [VMEM] * (4 + len(c)) + [ANY] * len(behind),
            (one,) * len(c),
            "middle",
        )
        for q, total in zip(c, added):
            totals[q] = total
        behind = added[:1]
    totals = call(
        functools.partial(first_kernel, undo),
        (*fixed, vmem(first), *totals),
        [VMEM] * 7,
        (one,) * 3,
        "first",
    )
    return call(
        functools.partial(last_kernel, undo, pieces[-1][1]),
        (*fixed, vmem(second[-1]), *totals),
        [VMEM] * 7,
        whole,
        "last",
        out_specs=ANY,
        scratch_shapes=[pltpu.VMEM(shape[1:], jnp.float32), pltpu.SemaphoreType.DMA((5,))],
    )


def solution(mesh):
    spec = P(None, "gx", "gy", None)
    body = functools.partial(shards, mesh.shape["gy"])
    return jax.shard_map(body, mesh=mesh, in_specs=(spec, spec), out_specs=spec, check_vma=False)
```

```python
import functools

import jax
import jax.numpy as jnp
import numpy as np
from jax import lax
from jax.experimental import pallas as pl
from jax.experimental.pallas import tpu as pltpu
from jax.sharding import PartitionSpec as P

NY = 1024


LENGTH_SPACING = 8.0 * 3.141592653589793 / 4096.0
SPAN_SPACING = 3.0 * 3.141592653589793 / 3072.0
VISCOSITY = 1.0 / 2000.0
TIME_STEP = 0.003
GAMMA_NOW = 5.0 / 12.0
ZETA_PAST = -17.0 / 60.0

SCALE = TIME_STEP * GAMMA_NOW
X_FIRST = SCALE / (12.0 * LENGTH_SPACING)
X_SECOND = SCALE * VISCOSITY / (12.0 * LENGTH_SPACING * LENGTH_SPACING)
Z_FIRST = SCALE / (12.0 * SPAN_SPACING)
Z_SECOND = SCALE * VISCOSITY / (12.0 * SPAN_SPACING * SPAN_SPACING)
PAST = TIME_STEP * ZETA_PAST

VMEM_LIMIT = 24 * 1024 * 1024
PIECES = ((0, 1), (2,))
LAST = 2
TILE = 32
COARSE_LARGEST = 224.0
COARSE_LIFT = 32.0
LOW_LIFT = 512.0


def chebyshev_matrices(total):
    one = np.float32(1.0)
    ids = np.arange(total, dtype=np.int32)
    angle = ids.astype(np.float32) * (np.float32(np.pi) / np.float32(total - 1))
    on_diagonal = ids[:, None] == ids[None, :]
    signs = one - np.float32(2.0) * ((ids[:, None] + ids[None, :]) % 2).astype(np.float32)
    half = np.where((ids == 0) | (ids == total - 1), 0.5, 1.0).astype(np.float32)
    weight_ratio = signs * half[None, :] / half[:, None]
    spacing = (
        np.float32(-2.0)
        * np.sin(np.float32(0.5) * (angle[:, None] + angle[None, :]))
        * np.sin(np.float32(0.5) * (angle[:, None] - angle[None, :]))
    )
    spacing = np.where(on_diagonal, one, spacing)
    first = np.where(on_diagonal, np.float32(0.0), weight_ratio / spacing)
    first_diag = -np.sum(first, axis=1, dtype=np.float32)
    second = np.where(
        on_diagonal,
        np.float32(0.0),
        np.float32(2.0) * first * (first_diag[:, None] - one / spacing),
    )
    second_diag = -np.sum(second, axis=1, dtype=np.float32)
    first[ids, ids] = first_diag
    second[ids, ids] = second_diag
    return first, second


def operator_blocks(total, parts):
    first, second = chebyshev_matrices(total)
    rows = total // parts
    stacked = np.stack(
        [first.astype(np.float64) * SCALE, second.astype(np.float64) * (SCALE * VISCOSITY)]
    ).astype(np.float32)
    blocks = stacked.reshape(2, parts, rows, parts, rows).transpose(1, 3, 0, 2, 4)
    mine = np.arange(parts)
    own = blocks[mine, mine]
    there = np.stack([blocks[mine, (mine - k) % parts] for k in range(1, parts)], axis=1)
    largest = np.max(np.abs(there), axis=(0, 1, 3, 4))
    scale = np.exp2(np.floor(np.log2(COARSE_LARGEST / largest))).astype(np.float32)
    own = own.reshape(parts, 2 * rows, rows)
    high = own.astype(jnp.bfloat16)
    own = np.stack([high, (own - high.astype(np.float32)).astype(jnp.bfloat16)], axis=1)
    high = there.astype(jnp.bfloat16)
    low = there - high.astype(np.float32)
    coarse = np.concatenate([LOW_LIFT * low, there], axis=-1) * scale[:, None, None]
    coarse = coarse.astype(jnp.float8_e4m3fn)
    shape = (parts, parts - 1, 2 * rows)
    undo = [float(1.0 / (x * LOW_LIFT * COARSE_LIFT)) for x in scale]
    return own, high.reshape(shape + (rows,)), coarse.reshape(shape + (2 * rows,)), undo


def wall(operators, fields, v):
    rows = v.shape[1]
    side = jnp.concatenate([fields[0], fields[1]], axis=1)
    high = side.astype(jnp.bfloat16)
    low = (side - high.astype(jnp.float32)).astype(jnp.bfloat16)
    dot = functools.partial(jnp.dot, preferred_element_type=jnp.float32)
    product = dot(operators[0], high) + (dot(operators[1], high) + dot(operators[0], low))
    first, second = product[:rows], product[rows:]
    added = second - jnp.concatenate([v[0], v[1]], axis=1) * first
    return added[:, : v.shape[2]], added[:, v.shape[2] :]


def second_pieces(rows):
    early = rows * 3 // 4 if rows % 512 == 0 else rows
    pieces = [((0, 1), 0, rows), ((LAST,), 0, early), ((LAST,), early, rows - early)]
    return [piece for piece in pieces if piece[2]]


def parted_field(fields):
    side = jnp.concatenate([fields[0], fields[1]], axis=1)
    high = side.astype(jnp.bfloat16)
    low = side - high.astype(jnp.float32)
    values = (COARSE_LIFT * side).astype(jnp.float8_e4m3fn)
    return high, values, (LOW_LIFT * COARSE_LIFT * low).astype(jnp.float8_e4m3fn)


def wall_rows(undo, operators, field, v, start, count, begin=0):
    rows = v.shape[1]
    (high_operators, coarse_operators), (high, values, lows) = operators, field
    depth = high.shape[0]
    dot = functools.partial(jnp.dot, preferred_element_type=jnp.float32)
    sums = []
    for matrix in range(2):
        at = pl.ds(matrix * rows + start, count)
        product = dot(high_operators[at, begin : begin + depth], high)
        if depth == rows:
            rest = dot(coarse_operators[at], jnp.concatenate([values, lows], axis=0))
        else:
            rest = dot(coarse_operators[at, begin : begin + depth], values)
            rest += dot(coarse_operators[at, rows + begin : rows + begin + depth], lows)
        sums.append(product + undo[matrix] * rest)
    at = pl.ds(start, count)
    added = sums[1] - jnp.concatenate([v[0, at], v[1, at]], axis=1) * sums[0]
    return added[:, : v.shape[2]], added[:, v.shape[2] :]


def wall_there(undo, high_operators, coarse_operators, fields, v, begin=0):
    operators = (high_operators, coarse_operators)
    return wall_rows(undo, operators, parted_field(fields), v, 0, v.shape[1], begin)


def along_x(parity):
    return jnp.where(parity == 0, X_FIRST, -X_FIRST).astype(jnp.float32)


def local_kernel(cuts, blocks, velocity, previous, *refs):
    outs, parted, (own, past, operators, came, sent) = refs[:3], refs[3:-5], refs[-5:]
    me = lax.axis_index("gy")
    fetches = [
        pltpu.make_async_copy(velocity, own, came.at[0]),
        pltpu.make_async_copy(blocks.at[me], operators, came.at[1]),
        pltpu.make_async_copy(previous, past, came.at[2]),
    ]
    for fetch in fetches:
        fetch.start()
    fetches[0].wait()
    stores = [
        pltpu.make_async_copy(own.at[c[0] : c[-1] + 1, :, pl.ds(begin, count)], part, sent.at[i])
        for i, ((c, begin, count), part) in enumerate(zip(cuts, parted))
    ]
    for store in stores:
        store.start()
    for fetch in fetches[1:]:
        fetch.wait()
    width = own.shape[3]
    roll = lambda f, k: pltpu.roll(f, k % width, 1)
    for q in range(3):
        added = wall(operators, own[q], own[1])
        for plane in range(2):
            f, other = own[q, plane], own[q, 1 - plane]
            u, w = own[0, plane], own[2, plane]
            step = X_FIRST if plane == 0 else -X_FIRST
            total = X_SECOND * (16.0 * other - 30.0 * f) - u * ((8.0 * step) * other)
            p1, m1, p2, m2 = roll(f, -1), roll(f, 1), roll(f, -2), roll(f, 2)
            total += Z_SECOND * (16.0 * (p1 + m1) - (p2 + m2) - 30.0 * f)
            total -= w * (Z_FIRST * (8.0 * (p1 - m1) - (p2 - m2)))
            outs[q][plane] = f + PAST * past[q, plane] + (total + added[plane])
    for store in stores:
        store.wait()


def near_kernel(velocity, *refs):
    near, refs = refs[: len(PIECES)], refs[len(PIECES) :]
    bases, outs, (u, slab, came) = refs[:3], refs[3:6], refs[6:]
    parity = lax.axis_index("gx") % 2
    inner, outer = 1 - parity, parity
    along = along_x(parity)
    fetches = [
        pltpu.make_async_copy(part.at[i], slab.at[q], came.at[q])
        for c, part in zip(PIECES, near)
        for i, q in enumerate(c)
    ]
    fetches.append(pltpu.make_async_copy(velocity.at[0], u, came.at[3]))
    for fetch in fetches:
        fetch.start()
    fetches[3].wait()
    for q in range(3):
        fetches[q].wait()
        base, out = bases[q], outs[q]
        first, second = slab[q, parity], slab[q, 1 - parity]
        out[outer] = base[outer] - X_SECOND * first + (along * u[outer]) * first
        out[inner] = (
            base[inner]
            + X_SECOND * (16.0 * first - second)
            - (along * u[inner]) * (8.0 * first - second)
        )


def far_terms(u):
    parity = lax.axis_index("gx") % 2
    inner, outer = 1 - parity, parity
    along = along_x(parity)
    inner_first = along * u[inner] + X_SECOND
    outer_second = along * u[outer] + X_SECOND
    outer_first = 8.0 * (outer_second + X_SECOND)

    def terms(far):
        first, second = far[1 - parity], far[parity]
        return (inner, -(inner_first * first)), (outer, outer_first * first - outer_second * second)

    return terms


def add(base, out, *terms):
    for plane, term in terms:
        out[plane] = base[plane] + term


def far_first(place):
    return (place + 1) // 2 % 2 == 1


def remote_kernel(undo, high_operators, coarse_operators, velocity, others, *refs):
    for q in range(3):
        terms = wall_there(undo, high_operators, coarse_operators, others[q], velocity.at[1])
        add(refs[q], refs[3 + q], *enumerate(terms))


def middle_kernel(undo, begin, count, high_operators, coarse_operators, velocity, piece, *refs):
    bases, outs = refs[:count], refs[-count:]
    swapped = far_first(lax.axis_index("gx"))
    at = pl.ds(begin, piece.shape[2])

    @pl.when(swapped)
    def _():
        for i, (base, out) in enumerate(zip(bases, outs)):
            terms = wall_there(
                undo, high_operators, coarse_operators, piece[i], velocity.at[1], begin
            )
            add(base, out, *enumerate(terms))

    @pl.when(jnp.logical_not(swapped))
    def _():
        terms = far_terms(velocity.at[0, :, at])
        for i, (base, out) in enumerate(zip(bases, outs)):
            if piece.shape[2] < out.shape[1]:
                out[...] = base[...]
            add(base.at[:, at], out.at[:, at], *terms(piece.at[i]))


def first_kernel(undo, high_operators, coarse_operators, velocity, whole, *refs):
    bases, outs = refs[:3], refs[3:]
    swapped = far_first(lax.axis_index("gx"))

    @pl.when(swapped)
    def _():
        outs[LAST][...] = bases[LAST][...]
        for start in range(0, velocity.shape[2], TILE):
            at = pl.ds(start, TILE)
            terms = far_terms(velocity.at[0, :, at])
            for q in range(3):
                if q != LAST:
                    add(bases[q].at[:, at], outs[q].at[:, at], *terms(whole.at[q, :, at]))

    @pl.when(jnp.logical_not(swapped))
    def _():
        for q in range(3):
            terms = wall_there(undo, high_operators, coarse_operators, whole[q], velocity.at[1])
            add(bases[q], outs[q], *enumerate(terms))


def last_kernel(undo, begin, high_operators, coarse_operators, velocity, whole, piece, *refs):
    bases, (out, total, sent) = refs[:3], refs[3:]
    swapped = far_first(lax.axis_index("gx"))
    operators = (high_operators, coarse_operators)
    half = velocity.shape[2] // 2
    ready = [q for q in range(3) if q != LAST]
    stores = [pltpu.make_async_copy(bases[q], out.at[q], sent.at[q]) for q in ready]
    for store in stores:
        store.start()
    for i in range(2):
        at = pl.ds(i * half, half)
        stores.append(pltpu.make_async_copy(total.at[:, at], out.at[LAST, :, at], sent.at[3 + i]))

    @pl.when(swapped)
    def _():
        field = parted_field(piece[0])
        for i in range(2):
            at = pl.ds(i * half, half)
            terms = far_terms(velocity.at[0, :, at])
            add(bases[LAST].at[:, at], total.at[:, at], *terms(whole.at[LAST, :, at]))
            more = wall_rows(undo, operators, field, velocity.at[1], i * half, half, begin)
            for plane in range(2):
                total[plane, at] += more[plane]
            stores[2 + i].start()

    @pl.when(jnp.logical_not(swapped))
    def _():
        at = pl.ds(begin, piece.shape[2])
        total[...] = bases[LAST][...]
        terms = far_terms(velocity.at[0, :, at])
        add(bases[LAST].at[:, at], total.at[:, at], *terms(piece.at[0]))
        for i in range(2):
            stores[2 + i].start()

    for store in stores:
        store.wait()


VMEM = pl.BlockSpec(memory_space=pltpu.VMEM)
ANY = pl.BlockSpec(memory_space=pl.ANY)


def vmem(array):
    return pltpu.with_memory_space_constraint(array, pltpu.VMEM)


def hbm(array):
    return pltpu.with_memory_space_constraint(array, pltpu.HBM)


def call(kernel, ins, in_specs, out_shape, name, **kwargs):
    kwargs.setdefault("out_specs", jax.tree.map(lambda _: VMEM, out_shape))
    return pl.pallas_call(
        kernel,
        in_specs=in_specs,
        out_shape=out_shape,
        compiler_params=pltpu.CompilerParams(vmem_limit_bytes=VMEM_LIMIT),
        cost_estimate=pl.CostEstimate(flops=0, bytes_accessed=0, transcendentals=0),
        name=name,
        **kwargs,
    )(*ins)


def shards(parts, velocity, previous):
    count = lax.axis_size("gx")
    shape = velocity.shape
    assert shape[0] == 3 and shape[1] == 2 and count % 4 == 0
    rows = shape[2]
    me = lax.axis_index("gy")

    inward = [(i, i ^ 1) for i in range(count)]
    firsts, seconds = [], []
    for g in range(count):
        beyond = (g - 1) % count if g % 2 == 0 else (g + 1) % count
        for i in range(parts):
            here = g * parts + i
            pair = [(here, beyond * parts + i), (here, g * parts + (i + 1) % parts)]
            firsts.append(pair[0] if far_first(g) else pair[1])
            seconds.append(pair[1] if far_first(g) else pair[0])
    both = ("gx", "gy")
    first = lax.ppermute(velocity, both, firsts)
    others = [
        lax.ppermute(velocity, "gy", [(i, (i + k) % parts) for i in range(parts)])
        for k in range(2, parts)
    ]

    own, high, coarse, undo = operator_blocks(rows * parts, parts)
    own = jnp.asarray(own)
    high = lax.dynamic_index_in_dim(jnp.asarray(high), me, 0, keepdims=False)
    coarse = lax.dynamic_index_in_dim(jnp.asarray(coarse), me, 0, keepdims=False)

    one = jax.ShapeDtypeStruct(shape[1:], jnp.float32)
    whole = jax.ShapeDtypeStruct(shape, jnp.float32)
    pieces = second_pieces(rows)
    cuts = [(c, 0, rows) for c in PIECES]
    cuts += [piece for piece in pieces if piece not in cuts]
    made = call(
        functools.partial(local_kernel, cuts),
        (hbm(own), hbm(velocity), hbm(previous)),
        [ANY] * 3,
        (one,) * 3
        + tuple(
            jax.ShapeDtypeStruct((len(c), shape[1], n, shape[3]), jnp.float32) for c, _, n in cuts
        ),
        "local",
        out_specs=(VMEM,) * 3 + (ANY,) * len(cuts),
        scratch_shapes=[
            pltpu.VMEM(shape, jnp.float32),
            pltpu.VMEM(shape, jnp.float32),
            pltpu.VMEM(own.shape[1:], jnp.bfloat16),
            pltpu.SemaphoreType.DMA((3,)),
            pltpu.SemaphoreType.DMA((len(cuts),)),
        ],
    )
    totals, parted = made[:3], made[3:]
    near = [lax.ppermute(part, "gx", inward) for part in parted[: len(PIECES)]]
    second = [lax.ppermute(parted[cuts.index(piece)], both, seconds) for piece in pieces]
    totals = call(
        near_kernel,
        (hbm(velocity), *map(hbm, near), *totals),
        [ANY] * (1 + len(PIECES)) + [VMEM] * 3,
        (one,) * 3,
        "near",
        scratch_shapes=[
            pltpu.VMEM(shape[1:], jnp.float32),
            pltpu.VMEM(shape, jnp.float32),
            pltpu.SemaphoreType.DMA((4,)),
        ],
    )
    for k in range(2, parts):
        totals = call(
            functools.partial(remote_kernel, undo),
            (high[k - 1], coarse[k - 1], velocity, others[k - 2], *totals),
            [VMEM] * 7,
            (one,) * 3,
            "remote",
        )
    totals = list(totals)
    fixed = (vmem(high[0]), vmem(coarse[0]), vmem(velocity))
    behind = ()
    for (c, begin, _), piece in zip(pieces[:-1], second):
        added = call(
            functools.partial(middle_kernel, undo, begin, len(c)),
            (*fixed, piece, *(totals[q] for q in c), *behind),
            [VMEM] * (4 + len(c)) + [ANY] * len(behind),
            (one,) * len(c),
            "middle",
        )
        for q, total in zip(c, added):
            totals[q] = total
        behind = added[:1]
    totals = call(
        functools.partial(first_kernel, undo),
        (*fixed, vmem(first), *totals),
        [VMEM] * 7,
        (one,) * 3,
        "first",
    )
    return call(
        functools.partial(last_kernel, undo, pieces[-1][1]),
        (*fixed, vmem(first), vmem(second[-1]), *totals),
        [VMEM] * 8,
        whole,
        "last",
        out_specs=ANY,
        scratch_shapes=[pltpu.VMEM(shape[1:], jnp.float32), pltpu.SemaphoreType.DMA((5,))],
    )


def solution(mesh):
    spec = P(None, "gx", "gy", None)
    body = functools.partial(shards, mesh.shape["gy"])
    return jax.shard_map(body, mesh=mesh, in_specs=(spec, spec), out_specs=spec, check_vma=False)
```

```python
import functools

import jax
import jax.numpy as jnp
import numpy as np
from jax import lax
from jax.experimental import pallas as pl
from jax.experimental.pallas import tpu as pltpu
from jax.sharding import PartitionSpec as P

NY = 1024


LENGTH_SPACING = 8.0 * 3.141592653589793 / 4096.0
SPAN_SPACING = 3.0 * 3.141592653589793 / 3072.0
VISCOSITY = 1.0 / 2000.0
TIME_STEP = 0.003
GAMMA_NOW = 5.0 / 12.0
ZETA_PAST = -17.0 / 60.0

SCALE = TIME_STEP * GAMMA_NOW
X_FIRST = SCALE / (12.0 * LENGTH_SPACING)
X_SECOND = SCALE * VISCOSITY / (12.0 * LENGTH_SPACING * LENGTH_SPACING)
Z_FIRST = SCALE / (12.0 * SPAN_SPACING)
Z_SECOND = SCALE * VISCOSITY / (12.0 * SPAN_SPACING * SPAN_SPACING)
PAST = TIME_STEP * ZETA_PAST

VMEM_LIMIT = 24 * 1024 * 1024
PIECES = ((0, 1), (2,))
LAST = 2
TILE = 32
COARSE_LARGEST = 224.0
COARSE_LIFT = 32.0
LOW_LIFT = 512.0


def chebyshev_matrices(total):
    one = np.float32(1.0)
    ids = np.arange(total, dtype=np.int32)
    angle = ids.astype(np.float32) * (np.float32(np.pi) / np.float32(total - 1))
    on_diagonal = ids[:, None] == ids[None, :]
    signs = one - np.float32(2.0) * ((ids[:, None] + ids[None, :]) % 2).astype(np.float32)
    half = np.where((ids == 0) | (ids == total - 1), 0.5, 1.0).astype(np.float32)
    weight_ratio = signs * half[None, :] / half[:, None]
    spacing = (
        np.float32(-2.0)
        * np.sin(np.float32(0.5) * (angle[:, None] + angle[None, :]))
        * np.sin(np.float32(0.5) * (angle[:, None] - angle[None, :]))
    )
    spacing = np.where(on_diagonal, one, spacing)
    first = np.where(on_diagonal, np.float32(0.0), weight_ratio / spacing)
    first_diag = -np.sum(first, axis=1, dtype=np.float32)
    second = np.where(
        on_diagonal,
        np.float32(0.0),
        np.float32(2.0) * first * (first_diag[:, None] - one / spacing),
    )
    second_diag = -np.sum(second, axis=1, dtype=np.float32)
    first[ids, ids] = first_diag
    second[ids, ids] = second_diag
    return first, second


def operator_blocks(total, parts):
    first, second = chebyshev_matrices(total)
    rows = total // parts
    stacked = np.stack(
        [first.astype(np.float64) * SCALE, second.astype(np.float64) * (SCALE * VISCOSITY)]
    ).astype(np.float32)
    blocks = stacked.reshape(2, parts, rows, parts, rows).transpose(1, 3, 0, 2, 4)
    mine = np.arange(parts)
    own = blocks[mine, mine]
    there = np.stack([blocks[mine, (mine - k) % parts] for k in range(1, parts)], axis=1)
    largest = np.max(np.abs(there), axis=(0, 1, 3, 4))
    scale = np.exp2(np.floor(np.log2(COARSE_LARGEST / largest))).astype(np.float32)
    own = own.reshape(parts, 2 * rows, rows)
    high = own.astype(jnp.bfloat16)
    own = np.stack([high, (own - high.astype(np.float32)).astype(jnp.bfloat16)], axis=1)
    high = there.astype(jnp.bfloat16)
    low = there - high.astype(np.float32)
    coarse = np.concatenate([LOW_LIFT * low, there], axis=-1) * scale[:, None, None]
    coarse = coarse.astype(jnp.float8_e4m3fn)
    shape = (parts, parts - 1, 2 * rows)
    undo = [float(1.0 / (x * LOW_LIFT * COARSE_LIFT)) for x in scale]
    return own, high.reshape(shape + (rows,)), coarse.reshape(shape + (2 * rows,)), undo


def wall(operators, fields, v):
    rows = v.shape[1]
    side = jnp.concatenate([fields[0], fields[1]], axis=1)
    high = side.astype(jnp.bfloat16)
    low = (side - high.astype(jnp.float32)).astype(jnp.bfloat16)
    dot = functools.partial(jnp.dot, preferred_element_type=jnp.float32)
    product = dot(operators[0], high) + (dot(operators[1], high) + dot(operators[0], low))
    first, second = product[:rows], product[rows:]
    added = second - jnp.concatenate([v[0], v[1]], axis=1) * first
    return added[:, : v.shape[2]], added[:, v.shape[2] :]


def second_pieces(rows):
    early = rows * 3 // 4 if rows % 512 == 0 else rows
    pieces = [((0, 1), 0, rows), ((LAST,), 0, early), ((LAST,), early, rows - early)]
    return [piece for piece in pieces if piece[2]]


def parted_field(fields):
    side = jnp.concatenate([fields[0], fields[1]], axis=1)
    high = side.astype(jnp.bfloat16)
    low = side - high.astype(jnp.float32)
    values = (COARSE_LIFT * side).astype(jnp.float8_e4m3fn)
    return high, values, (LOW_LIFT * COARSE_LIFT * low).astype(jnp.float8_e4m3fn)


def wall_rows(undo, operators, field, v, start, count, begin=0):
    rows = v.shape[1]
    (high_operators, coarse_operators), (high, values, lows) = operators, field
    depth = high.shape[0]
    dot = functools.partial(jnp.dot, preferred_element_type=jnp.float32)
    sums = []
    for matrix in range(2):
        at = pl.ds(matrix * rows + start, count)
        product = dot(high_operators[at, begin : begin + depth], high)
        if depth == rows:
            rest = dot(coarse_operators[at], jnp.concatenate([values, lows], axis=0))
        else:
            rest = dot(coarse_operators[at, begin : begin + depth], values)
            rest += dot(coarse_operators[at, rows + begin : rows + begin + depth], lows)
        sums.append(product + undo[matrix] * rest)
    at = pl.ds(start, count)
    added = sums[1] - jnp.concatenate([v[0, at], v[1, at]], axis=1) * sums[0]
    return added[:, : v.shape[2]], added[:, v.shape[2] :]


def wall_there(undo, high_operators, coarse_operators, fields, v, begin=0):
    operators = (high_operators, coarse_operators)
    return wall_rows(undo, operators, parted_field(fields), v, 0, v.shape[1], begin)


def along_x(parity):
    return jnp.where(parity == 0, X_FIRST, -X_FIRST).astype(jnp.float32)


def local_kernel(cuts, blocks, velocity, previous, *refs):
    outs, parted, (own, past, operators, came, sent) = refs[:3], refs[3:-5], refs[-5:]
    me = lax.axis_index("gy")
    fetches = [
        pltpu.make_async_copy(velocity, own, came.at[0]),
        pltpu.make_async_copy(blocks.at[me], operators, came.at[1]),
        pltpu.make_async_copy(previous, past, came.at[2]),
    ]
    for fetch in fetches:
        fetch.start()
    fetches[0].wait()
    stores = [
        pltpu.make_async_copy(own.at[c[0] : c[-1] + 1, :, pl.ds(begin, count)], part, sent.at[i])
        for i, ((c, begin, count), part) in enumerate(zip(cuts, parted))
    ]
    for store in stores:
        store.start()
    for fetch in fetches[1:]:
        fetch.wait()
    width = own.shape[3]
    roll = lambda f, k: pltpu.roll(f, k % width, 1)
    for q in range(3):
        added = wall(operators, own[q], own[1])
        for plane in range(2):
            f, other = own[q, plane], own[q, 1 - plane]
            u, w = own[0, plane], own[2, plane]
            step = X_FIRST if plane == 0 else -X_FIRST
            total = X_SECOND * (16.0 * other - 30.0 * f) - u * ((8.0 * step) * other)
            p1, m1, p2, m2 = roll(f, -1), roll(f, 1), roll(f, -2), roll(f, 2)
            total += Z_SECOND * (16.0 * (p1 + m1) - (p2 + m2) - 30.0 * f)
            total -= w * (Z_FIRST * (8.0 * (p1 - m1) - (p2 - m2)))
            outs[q][plane] = f + PAST * past[q, plane] + (total + added[plane])
    for store in stores:
        store.wait()


def near_kernel(velocity, *refs):
    near, refs = refs[: len(PIECES)], refs[len(PIECES) :]
    bases, outs, (u, slab, came) = refs[:3], refs[3:6], refs[6:]
    parity = lax.axis_index("gx") % 2
    inner, outer = 1 - parity, parity
    along = along_x(parity)
    fetches = [
        pltpu.make_async_copy(part.at[i], slab.at[q], came.at[q])
        for c, part in zip(PIECES, near)
        for i, q in enumerate(c)
    ]
    fetches.append(pltpu.make_async_copy(velocity.at[0], u, came.at[3]))
    for fetch in fetches:
        fetch.start()
    fetches[3].wait()
    for q in range(3):
        fetches[q].wait()
        base, out = bases[q], outs[q]
        first, second = slab[q, parity], slab[q, 1 - parity]
        out[outer] = base[outer] - X_SECOND * first + (along * u[outer]) * first
        out[inner] = (
            base[inner]
            + X_SECOND * (16.0 * first - second)
            - (along * u[inner]) * (8.0 * first - second)
        )


def far_terms(u):
    parity = lax.axis_index("gx") % 2
    inner, outer = 1 - parity, parity
    along = along_x(parity)
    inner_first = along * u[inner] + X_SECOND
    outer_second = along * u[outer] + X_SECOND
    outer_first = 8.0 * (outer_second + X_SECOND)

    def terms(far):
        first, second = far[1 - parity], far[parity]
        return (inner, -(inner_first * first)), (outer, outer_first * first - outer_second * second)

    return terms


def add(base, out, *terms):
    for plane, term in terms:
        out[plane] = base[plane] + term


def far_first(place):
    return (place + 1) // 2 % 2 == 1


def remote_kernel(undo, high_operators, coarse_operators, velocity, others, *refs):
    for q in range(3):
        terms = wall_there(undo, high_operators, coarse_operators, others[q], velocity.at[1])
        add(refs[q], refs[3 + q], *enumerate(terms))


def middle_kernel(undo, begin, count, high_operators, coarse_operators, velocity, piece, *refs):
    bases, outs = refs[:count], refs[-count:]
    swapped = far_first(lax.axis_index("gx"))
    at = pl.ds(begin, piece.shape[2])

    @pl.when(swapped)
    def _():
        for i, (base, out) in enumerate(zip(bases, outs)):
            terms = wall_there(
                undo, high_operators, coarse_operators, piece[i], velocity.at[1], begin
            )
            add(base, out, *enumerate(terms))

    @pl.when(jnp.logical_not(swapped))
    def _():
        terms = far_terms(velocity.at[0, :, at])
        for i, (base, out) in enumerate(zip(bases, outs)):
            if piece.shape[2] < out.shape[1]:
                out[...] = base[...]
            add(base.at[:, at], out.at[:, at], *terms(piece.at[i]))


def first_kernel(undo, high_operators, coarse_operators, velocity, whole, *refs):
    bases, outs = refs[:3], refs[3:]
    swapped = far_first(lax.axis_index("gx"))

    @pl.when(swapped)
    def _():
        outs[LAST][...] = bases[LAST][...]
        for start in range(0, velocity.shape[2], TILE):
            at = pl.ds(start, TILE)
            terms = far_terms(velocity.at[0, :, at])
            for q in range(3):
                if q != LAST:
                    add(bases[q].at[:, at], outs[q].at[:, at], *terms(whole.at[q, :, at]))

    @pl.when(jnp.logical_not(swapped))
    def _():
        for q in range(3):
            terms = wall_there(undo, high_operators, coarse_operators, whole[q], velocity.at[1])
            add(bases[q], outs[q], *enumerate(terms))


def last_kernel(undo, begin, high_operators, coarse_operators, velocity, whole, piece, *refs):
    bases, (out, total, sent) = refs[:3], refs[3:]
    swapped = far_first(lax.axis_index("gx"))
    operators = (high_operators, coarse_operators)
    half = velocity.shape[2] // 2
    ready = [q for q in range(3) if q != LAST]
    stores = [pltpu.make_async_copy(bases[q], out.at[q], sent.at[q]) for q in ready]
    for store in stores:
        store.start()
    for i in range(2):
        at = pl.ds(i * half, half)
        stores.append(pltpu.make_async_copy(total.at[:, at], out.at[LAST, :, at], sent.at[3 + i]))

    @pl.when(swapped)
    def _():
        field = parted_field(piece[0])
        for i in range(2):
            at = pl.ds(i * half, half)
            terms = far_terms(velocity.at[0, :, at])
            add(bases[LAST].at[:, at], total.at[:, at], *terms(whole.at[LAST, :, at]))
            more = wall_rows(undo, operators, field, velocity.at[1], i * half, half, begin)
            for plane in range(2):
                total[plane, at] += more[plane]
            stores[2 + i].start(priority=1)

    @pl.when(jnp.logical_not(swapped))
    def _():
        at = pl.ds(begin, piece.shape[2])
        total[...] = bases[LAST][...]
        terms = far_terms(velocity.at[0, :, at])
        add(bases[LAST].at[:, at], total.at[:, at], *terms(piece.at[0]))
        for i in range(2):
            stores[2 + i].start(priority=1)

    for store in stores:
        store.wait()


VMEM = pl.BlockSpec(memory_space=pltpu.VMEM)
ANY = pl.BlockSpec(memory_space=pl.ANY)


def vmem(array):
    return pltpu.with_memory_space_constraint(array, pltpu.VMEM)


def hbm(array):
    return pltpu.with_memory_space_constraint(array, pltpu.HBM)


def call(kernel, ins, in_specs, out_shape, name, **kwargs):
    kwargs.setdefault("out_specs", jax.tree.map(lambda _: VMEM, out_shape))
    return pl.pallas_call(
        kernel,
        in_specs=in_specs,
        out_shape=out_shape,
        compiler_params=pltpu.CompilerParams(vmem_limit_bytes=VMEM_LIMIT),
        cost_estimate=pl.CostEstimate(flops=0, bytes_accessed=0, transcendentals=0),
        name=name,
        **kwargs,
    )(*ins)


def shards(parts, velocity, previous):
    count = lax.axis_size("gx")
    shape = velocity.shape
    assert shape[0] == 3 and shape[1] == 2 and count % 4 == 0
    rows = shape[2]
    me = lax.axis_index("gy")

    inward = [(i, i ^ 1) for i in range(count)]
    firsts, seconds = [], []
    for g in range(count):
        beyond = (g - 1) % count if g % 2 == 0 else (g + 1) % count
        for i in range(parts):
            here = g * parts + i
            pair = [(here, beyond * parts + i), (here, g * parts + (i + 1) % parts)]
            firsts.append(pair[0] if far_first(g) else pair[1])
            seconds.append(pair[1] if far_first(g) else pair[0])
    both = ("gx", "gy")
    first = lax.ppermute(velocity, both, firsts)
    others = [
        lax.ppermute(velocity, "gy", [(i, (i + k) % parts) for i in range(parts)])
        for k in range(2, parts)
    ]

    own, high, coarse, undo = operator_blocks(rows * parts, parts)
    own = jnp.asarray(own)
    high = lax.dynamic_index_in_dim(jnp.asarray(high), me, 0, keepdims=False)
    coarse = lax.dynamic_index_in_dim(jnp.asarray(coarse), me, 0, keepdims=False)

    one = jax.ShapeDtypeStruct(shape[1:], jnp.float32)
    whole = jax.ShapeDtypeStruct(shape, jnp.float32)
    pieces = second_pieces(rows)
    cuts = [(c, 0, rows) for c in PIECES]
    cuts += [piece for piece in pieces if piece not in cuts]
    made = call(
        functools.partial(local_kernel, cuts),
        (hbm(own), hbm(velocity), hbm(previous)),
        [ANY] * 3,
        (one,) * 3
        + tuple(
            jax.ShapeDtypeStruct((len(c), shape[1], n, shape[3]), jnp.float32) for c, _, n in cuts
        ),
        "local",
        out_specs=(VMEM,) * 3 + (ANY,) * len(cuts),
        scratch_shapes=[
            pltpu.VMEM(shape, jnp.float32),
            pltpu.VMEM(shape, jnp.float32),
            pltpu.VMEM(own.shape[1:], jnp.bfloat16),
            pltpu.SemaphoreType.DMA((3,)),
            pltpu.SemaphoreType.DMA((len(cuts),)),
        ],
    )
    totals, parted = made[:3], made[3:]
    near = [lax.ppermute(part, "gx", inward) for part in parted[: len(PIECES)]]
    second = [lax.ppermute(parted[cuts.index(piece)], both, seconds) for piece in pieces]
    totals = call(
        near_kernel,
        (hbm(velocity), *map(hbm, near), *totals),
        [ANY] * (1 + len(PIECES)) + [VMEM] * 3,
        (one,) * 3,
        "near",
        scratch_shapes=[
            pltpu.VMEM(shape[1:], jnp.float32),
            pltpu.VMEM(shape, jnp.float32),
            pltpu.SemaphoreType.DMA((4,)),
        ],
    )
    for k in range(2, parts):
        totals = call(
            functools.partial(remote_kernel, undo),
            (high[k - 1], coarse[k - 1], velocity, others[k - 2], *totals),
            [VMEM] * 7,
            (one,) * 3,
            "remote",
        )
    totals = list(totals)
    fixed = (vmem(high[0]), vmem(coarse[0]), vmem(velocity))
    behind = ()
    for (c, begin, _), piece in zip(pieces[:-1], second):
        added = call(
            functools.partial(middle_kernel, undo, begin, len(c)),
            (*fixed, piece, *(totals[q] for q in c), *behind),
            [VMEM] * (4 + len(c)) + [ANY] * len(behind),
            (one,) * len(c),
            "middle",
        )
        for q, total in zip(c, added):
            totals[q] = total
        behind = added[:1]
    totals = call(
        functools.partial(first_kernel, undo),
        (*fixed, vmem(first), *totals),
        [VMEM] * 7,
        (one,) * 3,
        "first",
    )
    return call(
        functools.partial(last_kernel, undo, pieces[-1][1]),
        (*fixed, vmem(first), vmem(second[-1]), *totals),
        [VMEM] * 8,
        whole,
        "last",
        out_specs=ANY,
        scratch_shapes=[pltpu.VMEM(shape[1:], jnp.float32), pltpu.SemaphoreType.DMA((5,))],
    )


def solution(mesh):
    spec = P(None, "gx", "gy", None)
    body = functools.partial(shards, mesh.shape["gy"])
    return jax.shard_map(body, mesh=mesh, in_specs=(spec, spec), out_specs=spec, check_vma=False)
```

```python
import functools

import jax
import jax.numpy as jnp
import numpy as np
from jax import lax
from jax.experimental import pallas as pl
from jax.experimental.pallas import tpu as pltpu
from jax.sharding import PartitionSpec as P

NY = 1024


LENGTH_SPACING = 8.0 * 3.141592653589793 / 4096.0
SPAN_SPACING = 3.0 * 3.141592653589793 / 3072.0
VISCOSITY = 1.0 / 2000.0
TIME_STEP = 0.003
GAMMA_NOW = 5.0 / 12.0
ZETA_PAST = -17.0 / 60.0

SCALE = TIME_STEP * GAMMA_NOW
X_FIRST = SCALE / (12.0 * LENGTH_SPACING)
X_SECOND = SCALE * VISCOSITY / (12.0 * LENGTH_SPACING * LENGTH_SPACING)
Z_FIRST = SCALE / (12.0 * SPAN_SPACING)
Z_SECOND = SCALE * VISCOSITY / (12.0 * SPAN_SPACING * SPAN_SPACING)
PAST = TIME_STEP * ZETA_PAST

VMEM_LIMIT = 24 * 1024 * 1024
PIECES = ((0, 1), (2,))
LAST = 2
TILE = 32
COARSE_LARGEST = 224.0
COARSE_LIFT = 32.0
LOW_LIFT = 512.0


def chebyshev_matrices(total):
    one = np.float32(1.0)
    ids = np.arange(total, dtype=np.int32)
    angle = ids.astype(np.float32) * (np.float32(np.pi) / np.float32(total - 1))
    on_diagonal = ids[:, None] == ids[None, :]
    signs = one - np.float32(2.0) * ((ids[:, None] + ids[None, :]) % 2).astype(np.float32)
    half = np.where((ids == 0) | (ids == total - 1), 0.5, 1.0).astype(np.float32)
    weight_ratio = signs * half[None, :] / half[:, None]
    spacing = (
        np.float32(-2.0)
        * np.sin(np.float32(0.5) * (angle[:, None] + angle[None, :]))
        * np.sin(np.float32(0.5) * (angle[:, None] - angle[None, :]))
    )
    spacing = np.where(on_diagonal, one, spacing)
    first = np.where(on_diagonal, np.float32(0.0), weight_ratio / spacing)
    first_diag = -np.sum(first, axis=1, dtype=np.float32)
    second = np.where(
        on_diagonal,
        np.float32(0.0),
        np.float32(2.0) * first * (first_diag[:, None] - one / spacing),
    )
    second_diag = -np.sum(second, axis=1, dtype=np.float32)
    first[ids, ids] = first_diag
    second[ids, ids] = second_diag
    return first, second


def operator_blocks(total, parts):
    first, second = chebyshev_matrices(total)
    rows = total // parts
    stacked = np.stack(
        [first.astype(np.float64) * SCALE, second.astype(np.float64) * (SCALE * VISCOSITY)]
    ).astype(np.float32)
    blocks = stacked.reshape(2, parts, rows, parts, rows).transpose(1, 3, 0, 2, 4)
    mine = np.arange(parts)
    own = blocks[mine, mine]
    there = np.stack([blocks[mine, (mine - k) % parts] for k in range(1, parts)], axis=1)
    largest = np.max(np.abs(there), axis=(0, 1, 3, 4))
    scale = np.exp2(np.floor(np.log2(COARSE_LARGEST / largest))).astype(np.float32)
    own = own.reshape(parts, 2 * rows, rows)
    high = own.astype(jnp.bfloat16)
    own = np.stack([high, (own - high.astype(np.float32)).astype(jnp.bfloat16)], axis=1)
    high = there.astype(jnp.bfloat16)
    low = there - high.astype(np.float32)
    coarse = np.concatenate([LOW_LIFT * low, there], axis=-1) * scale[:, None, None]
    coarse = coarse.astype(jnp.float8_e4m3fn)
    shape = (parts, parts - 1, 2 * rows)
    undo = [float(1.0 / (x * LOW_LIFT * COARSE_LIFT)) for x in scale]
    return own, high.reshape(shape + (rows,)), coarse.reshape(shape + (2 * rows,)), undo


def wall(operators, fields, v):
    rows = v.shape[1]
    side = jnp.concatenate([fields[0], fields[1]], axis=1)
    high = side.astype(jnp.bfloat16)
    low = (side - high.astype(jnp.float32)).astype(jnp.bfloat16)
    dot = functools.partial(jnp.dot, preferred_element_type=jnp.float32)
    product = dot(operators[0], high) + (dot(operators[1], high) + dot(operators[0], low))
    first, second = product[:rows], product[rows:]
    added = second - jnp.concatenate([v[0], v[1]], axis=1) * first
    return added[:, : v.shape[2]], added[:, v.shape[2] :]


def second_pieces(rows):
    early = rows * 3 // 4 if rows % 512 == 0 else rows
    pieces = [((0, 1), 0, rows), ((LAST,), 0, early), ((LAST,), early, rows - early)]
    return [piece for piece in pieces if piece[2]]


def parted_field(fields):
    side = jnp.concatenate([fields[0], fields[1]], axis=1)
    high = side.astype(jnp.bfloat16)
    low = side - high.astype(jnp.float32)
    values = (COARSE_LIFT * side).astype(jnp.float8_e4m3fn)
    return high, values, (LOW_LIFT * COARSE_LIFT * low).astype(jnp.float8_e4m3fn)


def wall_rows(undo, operators, field, v, start, count, begin=0):
    rows = v.shape[1]
    (high_operators, coarse_operators), (high, values, lows) = operators, field
    depth = high.shape[0]
    dot = functools.partial(jnp.dot, preferred_element_type=jnp.float32)
    sums = []
    for matrix in range(2):
        at = pl.ds(matrix * rows + start, count)
        product = dot(high_operators[at, begin : begin + depth], high)
        if depth == rows:
            rest = dot(coarse_operators[at], jnp.concatenate([values, lows], axis=0))
        else:
            rest = dot(coarse_operators[at, begin : begin + depth], values)
            rest += dot(coarse_operators[at, rows + begin : rows + begin + depth], lows)
        sums.append(product + undo[matrix] * rest)
    at = pl.ds(start, count)
    added = sums[1] - jnp.concatenate([v[0, at], v[1, at]], axis=1) * sums[0]
    return added[:, : v.shape[2]], added[:, v.shape[2] :]


def wall_there(undo, high_operators, coarse_operators, fields, v, begin=0):
    operators = (high_operators, coarse_operators)
    return wall_rows(undo, operators, parted_field(fields), v, 0, v.shape[1], begin)


def along_x(parity):
    return jnp.where(parity == 0, X_FIRST, -X_FIRST).astype(jnp.float32)


def local_kernel(cuts, blocks, velocity, previous, *refs):
    outs, parted, (own, past, operators, came, sent) = refs[:3], refs[3:-5], refs[-5:]
    me = lax.axis_index("gy")
    fetches = [
        pltpu.make_async_copy(velocity, own, came.at[0]),
        pltpu.make_async_copy(blocks.at[me], operators, came.at[1]),
        pltpu.make_async_copy(previous, past, came.at[2]),
    ]
    for fetch in fetches:
        fetch.start()
    fetches[0].wait()
    stores = [
        pltpu.make_async_copy(own.at[c[0] : c[-1] + 1, :, pl.ds(begin, count)], part, sent.at[i])
        for i, ((c, begin, count), part) in enumerate(zip(cuts, parted))
    ]
    for store in stores:
        store.start()
    for fetch in fetches[1:]:
        fetch.wait()
    width = own.shape[3]
    roll = lambda f, k: pltpu.roll(f, k % width, 1)
    for q in range(3):
        added = wall(operators, own[q], own[1])
        for plane in range(2):
            f, other = own[q, plane], own[q, 1 - plane]
            u, w = own[0, plane], own[2, plane]
            step = X_FIRST if plane == 0 else -X_FIRST
            total = X_SECOND * (16.0 * other - 30.0 * f) - u * ((8.0 * step) * other)
            p1, m1, p2, m2 = roll(f, -1), roll(f, 1), roll(f, -2), roll(f, 2)
            total += Z_SECOND * (16.0 * (p1 + m1) - (p2 + m2) - 30.0 * f)
            total -= w * (Z_FIRST * (8.0 * (p1 - m1) - (p2 - m2)))
            outs[q][plane] = f + PAST * past[q, plane] + (total + added[plane])
    for store in stores:
        store.wait()


def near_kernel(velocity, *refs):
    near, refs = refs[: len(PIECES)], refs[len(PIECES) :]
    bases, outs, (u, slab, came) = refs[:3], refs[3:6], refs[6:]
    parity = lax.axis_index("gx") % 2
    inner, outer = 1 - parity, parity
    along = along_x(parity)
    fetches = [
        pltpu.make_async_copy(part.at[i], slab.at[q], came.at[q])
        for c, part in zip(PIECES, near)
        for i, q in enumerate(c)
    ]
    fetches.append(pltpu.make_async_copy(velocity.at[0], u, came.at[3]))
    for fetch in fetches:
        fetch.start()
    fetches[3].wait()
    for q in range(3):
        fetches[q].wait()
        base, out = bases[q], outs[q]
        first, second = slab[q, parity], slab[q, 1 - parity]
        out[outer] = base[outer] - X_SECOND * first + (along * u[outer]) * first
        out[inner] = (
            base[inner]
            + X_SECOND * (16.0 * first - second)
            - (along * u[inner]) * (8.0 * first - second)
        )


def far_terms(u):
    parity = lax.axis_index("gx") % 2
    inner, outer = 1 - parity, parity
    along = along_x(parity)
    inner_first = along * u[inner] + X_SECOND
    outer_second = along * u[outer] + X_SECOND
    outer_first = 8.0 * (outer_second + X_SECOND)

    def terms(far):
        first, second = far[1 - parity], far[parity]
        return (inner, -(inner_first * first)), (outer, outer_first * first - outer_second * second)

    return terms


def add(base, out, *terms):
    for plane, term in terms:
        out[plane] = base[plane] + term


def far_first(place):
    return (place + 1) // 2 % 2 == 1


def remote_kernel(undo, high_operators, coarse_operators, velocity, others, *refs):
    for q in range(3):
        terms = wall_there(undo, high_operators, coarse_operators, others[q], velocity.at[1])
        add(refs[q], refs[3 + q], *enumerate(terms))


def middle_kernel(undo, begin, count, high_operators, coarse_operators, velocity, piece, *refs):
    bases, outs = refs[:count], refs[-count:]
    swapped = far_first(lax.axis_index("gx"))
    at = pl.ds(begin, piece.shape[2])

    @pl.when(swapped)
    def _():
        for i, (base, out) in enumerate(zip(bases, outs)):
            terms = wall_there(
                undo, high_operators, coarse_operators, piece[i], velocity.at[1], begin
            )
            add(base, out, *enumerate(terms))

    @pl.when(jnp.logical_not(swapped))
    def _():
        terms = far_terms(velocity.at[0, :, at])
        for i, (base, out) in enumerate(zip(bases, outs)):
            if piece.shape[2] < out.shape[1]:
                out[...] = base[...]
            add(base.at[:, at], out.at[:, at], *terms(piece.at[i]))


def first_kernel(undo, high_operators, coarse_operators, velocity, whole, *refs):
    bases, outs = refs[:3], refs[3:]
    swapped = far_first(lax.axis_index("gx"))

    @pl.when(swapped)
    def _():
        for start in range(0, velocity.shape[2], TILE):
            at = pl.ds(start, TILE)
            terms = far_terms(velocity.at[0, :, at])
            for q in range(3):
                if q != LAST:
                    add(bases[q].at[:, at], outs[q].at[:, at], *terms(whole.at[q, :, at]))

    @pl.when(jnp.logical_not(swapped))
    def _():
        for q in range(3):
            terms = wall_there(undo, high_operators, coarse_operators, whole[q], velocity.at[1])
            add(bases[q], outs[q], *enumerate(terms))


def last_kernel(undo, begin, high_operators, coarse_operators, velocity, whole, piece, ahead, *refs):
    bases, (out, total, sent) = refs[:3], refs[3:]
    swapped = far_first(lax.axis_index("gx"))
    operators = (high_operators, coarse_operators)
    half = velocity.shape[2] // 2
    ready = [q for q in range(3) if q != LAST]
    stores = [pltpu.make_async_copy(bases[q], out.at[q], sent.at[q]) for q in ready]
    for store in stores:
        store.start()
    for i in range(2):
        at = pl.ds(i * half, half)
        stores.append(pltpu.make_async_copy(total.at[:, at], out.at[LAST, :, at], sent.at[3 + i]))

    @pl.when(swapped)
    def _():
        field = parted_field(piece[0])
        for i in range(2):
            at = pl.ds(i * half, half)
            terms = far_terms(velocity.at[0, :, at])
            add(ahead.at[:, at], total.at[:, at], *terms(whole.at[LAST, :, at]))
            more = wall_rows(undo, operators, field, velocity.at[1], i * half, half, begin)
            for plane in range(2):
                total[plane, at] += more[plane]
            stores[2 + i].start()

    @pl.when(jnp.logical_not(swapped))
    def _():
        at = pl.ds(begin, piece.shape[2])
        total[...] = bases[LAST][...]
        terms = far_terms(velocity.at[0, :, at])
        add(bases[LAST].at[:, at], total.at[:, at], *terms(piece.at[0]))
        for i in range(2):
            stores[2 + i].start()

    for store in stores:
        store.wait()


VMEM = pl.BlockSpec(memory_space=pltpu.VMEM)
ANY = pl.BlockSpec(memory_space=pl.ANY)


def vmem(array):
    return pltpu.with_memory_space_constraint(array, pltpu.VMEM)


def hbm(array):
    return pltpu.with_memory_space_constraint(array, pltpu.HBM)


def call(kernel, ins, in_specs, out_shape, name, **kwargs):
    kwargs.setdefault("out_specs", jax.tree.map(lambda _: VMEM, out_shape))
    return pl.pallas_call(
        kernel,
        in_specs=in_specs,
        out_shape=out_shape,
        compiler_params=pltpu.CompilerParams(vmem_limit_bytes=VMEM_LIMIT),
        cost_estimate=pl.CostEstimate(flops=0, bytes_accessed=0, transcendentals=0),
        name=name,
        **kwargs,
    )(*ins)


def shards(parts, velocity, previous):
    count = lax.axis_size("gx")
    shape = velocity.shape
    assert shape[0] == 3 and shape[1] == 2 and count % 4 == 0
    rows = shape[2]
    me = lax.axis_index("gy")

    inward = [(i, i ^ 1) for i in range(count)]
    firsts, seconds = [], []
    for g in range(count):
        beyond = (g - 1) % count if g % 2 == 0 else (g + 1) % count
        for i in range(parts):
            here = g * parts + i
            pair = [(here, beyond * parts + i), (here, g * parts + (i + 1) % parts)]
            firsts.append(pair[0] if far_first(g) else pair[1])
            seconds.append(pair[1] if far_first(g) else pair[0])
    both = ("gx", "gy")
    first = lax.ppermute(velocity, both, firsts)
    others = [
        lax.ppermute(velocity, "gy", [(i, (i + k) % parts) for i in range(parts)])
        for k in range(2, parts)
    ]

    own, high, coarse, undo = operator_blocks(rows * parts, parts)
    own = jnp.asarray(own)
    high = lax.dynamic_index_in_dim(jnp.asarray(high), me, 0, keepdims=False)
    coarse = lax.dynamic_index_in_dim(jnp.asarray(coarse), me, 0, keepdims=False)

    one = jax.ShapeDtypeStruct(shape[1:], jnp.float32)
    whole = jax.ShapeDtypeStruct(shape, jnp.float32)
    pieces = second_pieces(rows)
    cuts = [(c, 0, rows) for c in PIECES]
    cuts += [piece for piece in pieces if piece not in cuts]
    made = call(
        functools.partial(local_kernel, cuts),
        (hbm(own), hbm(velocity), hbm(previous)),
        [ANY] * 3,
        (one,) * 3
        + tuple(
            jax.ShapeDtypeStruct((len(c), shape[1], n, shape[3]), jnp.float32) for c, _, n in cuts
        ),
        "local",
        out_specs=(VMEM,) * 3 + (ANY,) * len(cuts),
        scratch_shapes=[
            pltpu.VMEM(shape, jnp.float32),
            pltpu.VMEM(shape, jnp.float32),
            pltpu.VMEM(own.shape[1:], jnp.bfloat16),
            pltpu.SemaphoreType.DMA((3,)),
            pltpu.SemaphoreType.DMA((len(cuts),)),
        ],
    )
    totals, parted = made[:3], made[3:]
    near = [lax.ppermute(part, "gx", inward) for part in parted[: len(PIECES)]]
    second = [lax.ppermute(parted[cuts.index(piece)], both, seconds) for piece in pieces]
    totals = call(
        near_kernel,
        (hbm(velocity), *map(hbm, near), *totals),
        [ANY] * (1 + len(PIECES)) + [VMEM] * 3,
        (one,) * 3,
        "near",
        scratch_shapes=[
            pltpu.VMEM(shape[1:], jnp.float32),
            pltpu.VMEM(shape, jnp.float32),
            pltpu.SemaphoreType.DMA((4,)),
        ],
    )
    for k in range(2, parts):
        totals = call(
            functools.partial(remote_kernel, undo),
            (high[k - 1], coarse[k - 1], velocity, others[k - 2], *totals),
            [VMEM] * 7,
            (one,) * 3,
            "remote",
        )
    totals = list(totals)
    fixed = (vmem(high[0]), vmem(coarse[0]), vmem(velocity))
    behind = ()
    for (c, begin, _), piece in zip(pieces[:-1], second):
        added = call(
            functools.partial(middle_kernel, undo, begin, len(c)),
            (*fixed, piece, *(totals[q] for q in c), *behind),
            [VMEM] * (4 + len(c)) + [ANY] * len(behind),
            (one,) * len(c),
            "middle",
        )
        for q, total in zip(c, added):
            totals[q] = total
        behind = added[:1]
    ahead = totals[LAST]
    totals = call(
        functools.partial(first_kernel, undo),
        (*fixed, vmem(first), *totals),
        [VMEM] * 7,
        (one,) * 3,
        "first",
    )
    return call(
        functools.partial(last_kernel, undo, pieces[-1][1]),
        (*fixed, vmem(first), vmem(second[-1]), ahead, *totals),
        [VMEM] * 9,
        whole,
        "last",
        out_specs=ANY,
        scratch_shapes=[pltpu.VMEM(shape[1:], jnp.float32), pltpu.SemaphoreType.DMA((5,))],
    )


def solution(mesh):
    spec = P(None, "gx", "gy", None)
    body = functools.partial(shards, mesh.shape["gy"])
    return jax.shard_map(body, mesh=mesh, in_specs=(spec, spec), out_specs=spec, check_vma=False)
```

```python
import functools

import jax
import jax.numpy as jnp
import numpy as np
from jax import lax
from jax.experimental import pallas as pl
from jax.experimental.pallas import tpu as pltpu
from jax.sharding import PartitionSpec as P

NY = 1024


LENGTH_SPACING = 8.0 * 3.141592653589793 / 4096.0
SPAN_SPACING = 3.0 * 3.141592653589793 / 3072.0
VISCOSITY = 1.0 / 2000.0
TIME_STEP = 0.003
GAMMA_NOW = 5.0 / 12.0
ZETA_PAST = -17.0 / 60.0

SCALE = TIME_STEP * GAMMA_NOW
X_FIRST = SCALE / (12.0 * LENGTH_SPACING)
X_SECOND = SCALE * VISCOSITY / (12.0 * LENGTH_SPACING * LENGTH_SPACING)
Z_FIRST = SCALE / (12.0 * SPAN_SPACING)
Z_SECOND = SCALE * VISCOSITY / (12.0 * SPAN_SPACING * SPAN_SPACING)
PAST = TIME_STEP * ZETA_PAST

VMEM_LIMIT = 24 * 1024 * 1024
PIECES = ((0, 1), (2,))
LAST = 2
TILE = 32
COARSE_LARGEST = 224.0
COARSE_LIFT = 32.0
LOW_LIFT = 512.0


def chebyshev_matrices(total):
    one = np.float32(1.0)
    ids = np.arange(total, dtype=np.int32)
    angle = ids.astype(np.float32) * (np.float32(np.pi) / np.float32(total - 1))
    on_diagonal = ids[:, None] == ids[None, :]
    signs = one - np.float32(2.0) * ((ids[:, None] + ids[None, :]) % 2).astype(np.float32)
    half = np.where((ids == 0) | (ids == total - 1), 0.5, 1.0).astype(np.float32)
    weight_ratio = signs * half[None, :] / half[:, None]
    spacing = (
        np.float32(-2.0)
        * np.sin(np.float32(0.5) * (angle[:, None] + angle[None, :]))
        * np.sin(np.float32(0.5) * (angle[:, None] - angle[None, :]))
    )
    spacing = np.where(on_diagonal, one, spacing)
    first = np.where(on_diagonal, np.float32(0.0), weight_ratio / spacing)
    first_diag = -np.sum(first, axis=1, dtype=np.float32)
    second = np.where(
        on_diagonal,
        np.float32(0.0),
        np.float32(2.0) * first * (first_diag[:, None] - one / spacing),
    )
    second_diag = -np.sum(second, axis=1, dtype=np.float32)
    first[ids, ids] = first_diag
    second[ids, ids] = second_diag
    return first, second


def operator_blocks(total, parts):
    first, second = chebyshev_matrices(total)
    rows = total // parts
    stacked = np.stack(
        [first.astype(np.float64) * SCALE, second.astype(np.float64) * (SCALE * VISCOSITY)]
    ).astype(np.float32)
    blocks = stacked.reshape(2, parts, rows, parts, rows).transpose(1, 3, 0, 2, 4)
    mine = np.arange(parts)
    own = blocks[mine, mine]
    there = np.stack([blocks[mine, (mine - k) % parts] for k in range(1, parts)], axis=1)
    largest = np.max(np.abs(there), axis=(0, 1, 3, 4))
    scale = np.exp2(np.floor(np.log2(COARSE_LARGEST / largest))).astype(np.float32)
    own = own.reshape(parts, 2 * rows, rows)
    high = own.astype(jnp.bfloat16)
    own = np.stack([high, (own - high.astype(np.float32)).astype(jnp.bfloat16)], axis=1)
    high = there.astype(jnp.bfloat16)
    low = there - high.astype(np.float32)
    coarse = np.concatenate([LOW_LIFT * low, there], axis=-1) * scale[:, None, None]
    coarse = coarse.astype(jnp.float8_e4m3fn)
    shape = (parts, parts - 1, 2 * rows)
    undo = [float(1.0 / (x * LOW_LIFT * COARSE_LIFT)) for x in scale]
    return own, high.reshape(shape + (rows,)), coarse.reshape(shape + (2 * rows,)), undo


def wall(operators, fields, v):
    rows = v.shape[1]
    side = jnp.concatenate([fields[0], fields[1]], axis=1)
    high = side.astype(jnp.bfloat16)
    low = (side - high.astype(jnp.float32)).astype(jnp.bfloat16)
    dot = functools.partial(jnp.dot, preferred_element_type=jnp.float32)
    product = dot(operators[0], high) + (dot(operators[1], high) + dot(operators[0], low))
    first, second = product[:rows], product[rows:]
    added = second - jnp.concatenate([v[0], v[1]], axis=1) * first
    return added[:, : v.shape[2]], added[:, v.shape[2] :]


def second_pieces(rows):
    early = rows * 3 // 4 if rows % 512 == 0 else rows
    pieces = [((0, 1), 0, rows), ((LAST,), 0, early), ((LAST,), early, rows - early)]
    return [piece for piece in pieces if piece[2]]


def parted_field(fields):
    side = jnp.concatenate([fields[0], fields[1]], axis=1)
    high = side.astype(jnp.bfloat16)
    low = side - high.astype(jnp.float32)
    values = (COARSE_LIFT * side).astype(jnp.float8_e4m3fn)
    return high, values, (LOW_LIFT * COARSE_LIFT * low).astype(jnp.float8_e4m3fn)


def wall_rows(undo, operators, field, v, start, count, begin=0):
    rows = v.shape[1]
    (high_operators, coarse_operators), (high, values, lows) = operators, field
    depth = high.shape[0]
    dot = functools.partial(jnp.dot, preferred_element_type=jnp.float32)
    sums = []
    for matrix in range(2):
        at = pl.ds(matrix * rows + start, count)
        product = dot(high_operators[at, begin : begin + depth], high)
        if depth == rows:
            rest = dot(coarse_operators[at], jnp.concatenate([values, lows], axis=0))
        else:
            rest = dot(coarse_operators[at, begin : begin + depth], values)
            rest += dot(coarse_operators[at, rows + begin : rows + begin + depth], lows)
        sums.append(product + undo[matrix] * rest)
    at = pl.ds(start, count)
    added = sums[1] - jnp.concatenate([v[0, at], v[1, at]], axis=1) * sums[0]
    return added[:, : v.shape[2]], added[:, v.shape[2] :]


def wall_there(undo, high_operators, coarse_operators, fields, v, begin=0):
    operators = (high_operators, coarse_operators)
    return wall_rows(undo, operators, parted_field(fields), v, 0, v.shape[1], begin)


def along_x(parity):
    return jnp.where(parity == 0, X_FIRST, -X_FIRST).astype(jnp.float32)


def local_kernel(cuts, blocks, velocity, previous, *refs):
    outs, parted, (own, past, operators, came, sent) = refs[:3], refs[3:-5], refs[-5:]
    me = lax.axis_index("gy")
    fetches = [
        pltpu.make_async_copy(velocity, own, came.at[0]),
        pltpu.make_async_copy(blocks.at[me], operators, came.at[1]),
        pltpu.make_async_copy(previous, past, came.at[2]),
    ]
    for fetch in fetches:
        fetch.start()
    fetches[0].wait()
    stores = [
        pltpu.make_async_copy(own.at[c[0] : c[-1] + 1, :, pl.ds(begin, count)], part, sent.at[i])
        for i, ((c, begin, count), part) in enumerate(zip(cuts, parted))
    ]
    for store in stores:
        store.start()
    for fetch in fetches[1:]:
        fetch.wait()
    width = own.shape[3]
    roll = lambda f, k: pltpu.roll(f, k % width, 1)
    for q in range(3):
        added = wall(operators, own[q], own[1])
        for plane in range(2):
            f, other = own[q, plane], own[q, 1 - plane]
            u, w = own[0, plane], own[2, plane]
            step = X_FIRST if plane == 0 else -X_FIRST
            total = X_SECOND * (16.0 * other - 30.0 * f) - u * ((8.0 * step) * other)
            p1, m1, p2, m2 = roll(f, -1), roll(f, 1), roll(f, -2), roll(f, 2)
            total += Z_SECOND * (16.0 * (p1 + m1) - (p2 + m2) - 30.0 * f)
            total -= w * (Z_FIRST * (8.0 * (p1 - m1) - (p2 - m2)))
            outs[q][plane] = f + PAST * past[q, plane] + (total + added[plane])
    for store in stores:
        store.wait()


def near_kernel(velocity, *refs):
    near, refs = refs[: len(PIECES)], refs[len(PIECES) :]
    bases, outs, (u, slab, came) = refs[:3], refs[3:6], refs[6:]
    parity = lax.axis_index("gx") % 2
    inner, outer = 1 - parity, parity
    along = along_x(parity)
    fetches = [
        pltpu.make_async_copy(part.at[i], slab.at[q], came.at[q])
        for c, part in zip(PIECES, near)
        for i, q in enumerate(c)
    ]
    fetches.append(pltpu.make_async_copy(velocity.at[0], u, came.at[3]))
    for fetch in fetches:
        fetch.start()
    fetches[3].wait()
    for q in range(3):
        fetches[q].wait()
        base, out = bases[q], outs[q]
        first, second = slab[q, parity], slab[q, 1 - parity]
        out[outer] = base[outer] - X_SECOND * first + (along * u[outer]) * first
        out[inner] = (
            base[inner]
            + X_SECOND * (16.0 * first - second)
            - (along * u[inner]) * (8.0 * first - second)
        )


def far_terms(u):
    parity = lax.axis_index("gx") % 2
    inner, outer = 1 - parity, parity
    along = along_x(parity)
    inner_first = along * u[inner] + X_SECOND
    outer_second = along * u[outer] + X_SECOND
    outer_first = 8.0 * (outer_second + X_SECOND)

    def terms(far):
        first, second = far[1 - parity], far[parity]
        return (inner, -(inner_first * first)), (outer, outer_first * first - outer_second * second)

    return terms


def add(base, out, *terms):
    for plane, term in terms:
        out[plane] = base[plane] + term


def far_first(place):
    return (place + 1) // 2 % 2 == 1


def remote_kernel(undo, high_operators, coarse_operators, velocity, others, *refs):
    for q in range(3):
        terms = wall_there(undo, high_operators, coarse_operators, others[q], velocity.at[1])
        add(refs[q], refs[3 + q], *enumerate(terms))


def middle_kernel(undo, begin, count, high_operators, coarse_operators, velocity, piece, *refs):
    bases, outs = refs[:count], refs[-count:]
    swapped = far_first(lax.axis_index("gx"))
    at = pl.ds(begin, piece.shape[2])

    @pl.when(swapped)
    def _():
        for i, (base, out) in enumerate(zip(bases, outs)):
            terms = wall_there(
                undo, high_operators, coarse_operators, piece[i], velocity.at[1], begin
            )
            add(base, out, *enumerate(terms))

    @pl.when(jnp.logical_not(swapped))
    def _():
        terms = far_terms(velocity.at[0, :, at])
        for i, (base, out) in enumerate(zip(bases, outs)):
            if piece.shape[2] < out.shape[1]:
                out[...] = base[...]
            add(base.at[:, at], out.at[:, at], *terms(piece.at[i]))


def first_kernel(undo, high_operators, coarse_operators, velocity, whole, *refs):
    bases, outs = refs[:3], refs[3:]
    swapped = far_first(lax.axis_index("gx"))

    @pl.when(swapped)
    def _():
        for start in range(0, velocity.shape[2], TILE):
            at = pl.ds(start, TILE)
            terms = far_terms(velocity.at[0, :, at])
            for q in range(3):
                if q != LAST:
                    add(bases[q].at[:, at], outs[q].at[:, at], *terms(whole.at[q, :, at]))

    @pl.when(jnp.logical_not(swapped))
    def _():
        for q in range(3):
            terms = wall_there(undo, high_operators, coarse_operators, whole[q], velocity.at[1])
            add(bases[q], outs[q], *enumerate(terms))


def last_kernel(undo, begin, high_operators, coarse_operators, velocity, whole, piece, ahead, *refs):
    bases, (out, total, sent) = refs[:3], refs[3:]
    swapped = far_first(lax.axis_index("gx"))
    operators = (high_operators, coarse_operators)
    half = velocity.shape[2] // 2
    ready = [q for q in range(3) if q != LAST]
    stores = [pltpu.make_async_copy(bases[q], out.at[q], sent.at[q]) for q in ready]
    for store in stores:
        store.start()
    for i in range(2):
        at = pl.ds(i * half, half)
        stores.append(pltpu.make_async_copy(total.at[:, at], out.at[LAST, :, at], sent.at[3 + i]))

    @pl.when(swapped)
    def _():
        field = parted_field(piece[0])
        for i in range(2):
            at = pl.ds(i * half, half)
            terms = far_terms(velocity.at[0, :, at])
            add(ahead.at[:, at], total.at[:, at], *terms(whole.at[LAST, :, at]))
            more = wall_rows(undo, operators, field, velocity.at[1], i * half, half, begin)
            for plane in range(2):
                total[plane, at] += more[plane]
            stores[2 + i].start(priority=1)

    @pl.when(jnp.logical_not(swapped))
    def _():
        at = pl.ds(begin, piece.shape[2])
        total[...] = bases[LAST][...]
        terms = far_terms(velocity.at[0, :, at])
        add(bases[LAST].at[:, at], total.at[:, at], *terms(piece.at[0]))
        for i in range(2):
            stores[2 + i].start(priority=1)

    for store in stores:
        store.wait()


VMEM = pl.BlockSpec(memory_space=pltpu.VMEM)
ANY = pl.BlockSpec(memory_space=pl.ANY)


def vmem(array):
    return pltpu.with_memory_space_constraint(array, pltpu.VMEM)


def hbm(array):
    return pltpu.with_memory_space_constraint(array, pltpu.HBM)


def call(kernel, ins, in_specs, out_shape, name, **kwargs):
    kwargs.setdefault("out_specs", jax.tree.map(lambda _: VMEM, out_shape))
    return pl.pallas_call(
        kernel,
        in_specs=in_specs,
        out_shape=out_shape,
        compiler_params=pltpu.CompilerParams(vmem_limit_bytes=VMEM_LIMIT),
        cost_estimate=pl.CostEstimate(flops=0, bytes_accessed=0, transcendentals=0),
        name=name,
        **kwargs,
    )(*ins)


def shards(parts, velocity, previous):
    count = lax.axis_size("gx")
    shape = velocity.shape
    assert shape[0] == 3 and shape[1] == 2 and count % 4 == 0
    rows = shape[2]
    me = lax.axis_index("gy")

    inward = [(i, i ^ 1) for i in range(count)]
    firsts, seconds = [], []
    for g in range(count):
        beyond = (g - 1) % count if g % 2 == 0 else (g + 1) % count
        for i in range(parts):
            here = g * parts + i
            pair = [(here, beyond * parts + i), (here, g * parts + (i + 1) % parts)]
            firsts.append(pair[0] if far_first(g) else pair[1])
            seconds.append(pair[1] if far_first(g) else pair[0])
    both = ("gx", "gy")
    first = lax.ppermute(velocity, both, firsts)
    others = [
        lax.ppermute(velocity, "gy", [(i, (i + k) % parts) for i in range(parts)])
        for k in range(2, parts)
    ]

    own, high, coarse, undo = operator_blocks(rows * parts, parts)
    own = jnp.asarray(own)
    high = lax.dynamic_index_in_dim(jnp.asarray(high), me, 0, keepdims=False)
    coarse = lax.dynamic_index_in_dim(jnp.asarray(coarse), me, 0, keepdims=False)

    one = jax.ShapeDtypeStruct(shape[1:], jnp.float32)
    whole = jax.ShapeDtypeStruct(shape, jnp.float32)
    pieces = second_pieces(rows)
    cuts = [(c, 0, rows) for c in PIECES]
    cuts += [piece for piece in pieces if piece not in cuts]
    made = call(
        functools.partial(local_kernel, cuts),
        (hbm(own), hbm(velocity), hbm(previous)),
        [ANY] * 3,
        (one,) * 3
        + tuple(
            jax.ShapeDtypeStruct((len(c), shape[1], n, shape[3]), jnp.float32) for c, _, n in cuts
        ),
        "local",
        out_specs=(VMEM,) * 3 + (ANY,) * len(cuts),
        scratch_shapes=[
            pltpu.VMEM(shape, jnp.float32),
            pltpu.VMEM(shape, jnp.float32),
            pltpu.VMEM(own.shape[1:], jnp.bfloat16),
            pltpu.SemaphoreType.DMA((3,)),
            pltpu.SemaphoreType.DMA((len(cuts),)),
        ],
    )
    totals, parted = made[:3], made[3:]
    near = [lax.ppermute(part, "gx", inward) for part in parted[: len(PIECES)]]
    second = [lax.ppermute(parted[cuts.index(piece)], both, seconds) for piece in pieces]
    totals = call(
        near_kernel,
        (hbm(velocity), *map(hbm, near), *totals),
        [ANY] * (1 + len(PIECES)) + [VMEM] * 3,
        (one,) * 3,
        "near",
        scratch_shapes=[
            pltpu.VMEM(shape[1:], jnp.float32),
            pltpu.VMEM(shape, jnp.float32),
            pltpu.SemaphoreType.DMA((4,)),
        ],
    )
    for k in range(2, parts):
        totals = call(
            functools.partial(remote_kernel, undo),
            (high[k - 1], coarse[k - 1], velocity, others[k - 2], *totals),
            [VMEM] * 7,
            (one,) * 3,
            "remote",
        )
    totals = list(totals)
    fixed = (vmem(high[0]), vmem(coarse[0]), vmem(velocity))
    behind = ()
    for (c, begin, _), piece in zip(pieces[:-1], second):
        added = call(
            functools.partial(middle_kernel, undo, begin, len(c)),
            (*fixed, piece, *(totals[q] for q in c), *behind),
            [VMEM] * (4 + len(c)) + [ANY] * len(behind),
            (one,) * len(c),
            "middle",
        )
        for q, total in zip(c, added):
            totals[q] = total
        behind = added[:1]
    ahead = totals[LAST]
    totals = call(
        functools.partial(first_kernel, undo),
        (*fixed, vmem(first), *totals),
        [VMEM] * 7,
        (one,) * 3,
        "first",
    )
    return call(
        functools.partial(last_kernel, undo, pieces[-1][1]),
        (*fixed, vmem(first), vmem(second[-1]), ahead, *totals),
        [VMEM] * 9,
        whole,
        "last",
        out_specs=ANY,
        scratch_shapes=[pltpu.VMEM(shape[1:], jnp.float32), pltpu.SemaphoreType.DMA((5,))],
    )


def solution(mesh):
    spec = P(None, "gx", "gy", None)
    body = functools.partial(shards, mesh.shape["gy"])
    return jax.shard_map(body, mesh=mesh, in_specs=(spec, spec), out_specs=spec, check_vma=False)
```
